128 devices in a mesh: row: 8 (over y, z_lo), col: 16 (over z_hi, x, core).
Axes of the slice: x: 4, y: 4, z: 4 (z_hi: 2, z_lo: 2; z = z_hi * 2 + z_lo), core: 2. Of those that a mesh axis runs over, the one named last changes fastest.
Arguments:
- fire_state: float32 [64, 384, 2048], P(None, 'row', 'col'), may hold values from -6 to 6
- fuel_class: int32 [384, 2048], P('row', 'col'), may hold values from 0 to 12
- firebreak: int32 [384, 2048], P('row', 'col'), may hold values 0 or 1
- ignition: int32 [384, 2048], P('row', 'col'), may hold values 0 or 1
- spread_rate: float32 [13, 64], replicated, may hold values from 0.03 to 0.12
- spread_rows: float32 [64, 64], replicated, may hold values from -0.375 to 0.375
- spread_cols: float32 [64, 64], replicated, may hold values from -0.375 to 0.375
- reaction: float32 [64, 64], replicated, may hold values from -0.75 to 0.75
- ignition_heat: float32 [64], replicated, may hold values from -4 to 4
Outputs:
- final_state: float32 [64, 384, 2048], P(None, 'row', 'col')
The draws below stay inside these ranges and needn't reach their ends.
All inputs are finite; a program needn't handle non-finite values. No bound on the sum of `firebreak` or of `ignition` on one device may be relied on, other than what follows from the above.
Results may differ from the reference program's by a relative error of at most 0.0003.
Values sent between devices are 32-bit elements; how exact they have to be, the bound alone decides.
No kernel may reach another device: no remote copies, remote signals or barrier semaphores. Data moves between devices by JAX's collectives and lax.ppermute only.
A program may use at most 64 MiB of HBM per device.

```python
import math
import jax
import jax.numpy as jnp
from jax import lax

C = 64
K = 13
W_DEV = 128
ITERS = 4
NX = 384
NY = 2048


def touch_ends(drawn, stream_key, low, largest):
    index_at = [jax.random.randint(jax.random.fold_in(stream_key, axis), (), 0, length) for axis, length in enumerate(drawn.shape)]
    main_axis = drawn.shape.index(max(drawn.shape))
    beside = index_at[:main_axis] + [(index_at[main_axis] + 1) % drawn.shape[main_axis]] + index_at[main_axis + 1:]
    return drawn.at[tuple(index_at)].set(low).at[tuple(beside)].set(largest)


def shard_levels(stream_key, dims, shards, smallest, high):
    gain = 1.0
    for axis_at, blocks in shards:
        heights = jax.random.uniform(jax.random.fold_in(jax.random.fold_in(stream_key, 6), axis_at), (blocks,), jnp.float32, smallest / len(shards), high / len(shards))
        gain = gain * jnp.repeat(jnp.exp(heights), dims[axis_at] // blocks).reshape((-1,) + (1,) * (len(dims) - 1 - axis_at))
    return gain


def centred(rng, dims, scale, reach, cuts=(), kind=jnp.bfloat16):
    array = jax.random.normal(rng, dims, jnp.float32) * scale
    if len(cuts) > 0:
        array = shard_levels(rng, dims, cuts, -0.22, 0.18) * array
    return jnp.clip(array, min=-reach, max=reach).astype(kind)


def setup_inputs(seed: int = 0) -> dict:
    key_list = jax.random.split(jax.random.key(seed), 10)
    fire_state = centred(key_list[0], (C, NX, NY), 1.0, 6.0, ((1, 8), (2, 16)), jnp.float32)
    fuel_class = touch_ends(jax.random.randint(key_list[1], (NX, NY), 0, K), jax.random.fold_in(key_list[1], 1), 0, K - 1).astype(jnp.int32)
    firebreak = touch_ends((jax.random.randint(key_list[2], (NX, NY), 0, 8) < 1).astype(jnp.int32), jax.random.fold_in(key_list[2], 1), 0, 1)
    ignition = touch_ends((jax.random.randint(key_list[3], (NX, NY), 0, 16) < 1).astype(jnp.int32), jax.random.fold_in(key_list[3], 1), 0, 1)
    spread_rate = jnp.clip(jnp.exp(jax.random.uniform(key_list[4], (K, C), jnp.float32, math.log(0.03), math.log(0.12))), 0.03, 0.12)
    spread_rows = centred(key_list[5], (C, C), (4 * C) ** -0.5, 0.375, (), jnp.float32)
    spread_cols = centred(key_list[6], (C, C), (4 * C) ** -0.5, 0.375, (), jnp.float32)
    reaction = centred(key_list[7], (C, C), C ** -0.5, 0.75, (), jnp.float32)
    ignition_heat = centred(key_list[8], (C,), 1.0, 4.0, (), jnp.float32)
    return dict(fire_state=fire_state, fuel_class=fuel_class, firebreak=firebreak, ignition=ignition, spread_rate=spread_rate, spread_rows=spread_rows, spread_cols=spread_cols, reaction=reaction, ignition_heat=ignition_heat)


def mixing(matrix, values):
    return jnp.einsum('dc,chw->dhw', matrix, values, precision=lax.Precision.HIGHEST)


def tendency(padded, burnable, spread, heating, spread_rows, spread_cols, reaction):
    center = padded[:, 1:-1, 1:-1]
    vertical = padded[:, :-2, 1:-1] + padded[:, 2:, 1:-1] - 2.0 * center
    horizontal = padded[:, 1:-1, :-2] + padded[:, 1:-1, 2:] - 2.0 * center
    mixed = vertical + mixing(spread_rows, vertical) + horizontal + mixing(spread_cols, horizontal)
    drive = spread * mixed + mixing(reaction, jnp.tanh(center)) + heating
    return burnable[None] * drive - 0.5 * center


def full_tendency(field, burnable_int, fuel_class, ignition, spread_rate, spread_rows, spread_cols, reaction, ignition_heat):
    padded = jnp.pad(field, ((0, 0), (1, 1), (1, 1)))
    blocks = NY // W_DEV

    def one_block(column_block):
        begin = column_block * W_DEV
        piece = lax.dynamic_slice_in_dim(padded, begin, W_DEV + 2, 2)
        burnable = lax.dynamic_slice_in_dim(burnable_int, begin, W_DEV, 1).astype(jnp.float32)
        fuel = lax.dynamic_slice_in_dim(fuel_class, begin, W_DEV, 1)
        lit = lax.dynamic_slice_in_dim(ignition, begin, W_DEV, 1).astype(jnp.float32)
        onehot = (fuel[None] == jnp.arange(K, dtype=jnp.int32)[:, None, None]).astype(jnp.float32)
        spread = jnp.einsum('kc,khw->chw', spread_rate, onehot, precision=lax.Precision.HIGHEST)
        heating = lit[None] * ignition_heat[:, None, None]
        return tendency(piece, burnable, spread, heating, spread_rows, spread_cols, reaction)

    result = lax.map(one_block, jnp.arange(blocks, dtype=jnp.int32))
    result = jnp.moveaxis(result, 0, 2)
    return result.reshape(C, NX, NY)


def reference(fire_state, fuel_class, firebreak, ignition, spread_rate, spread_rows, spread_cols, reaction, ignition_heat):
    burnable_int = 1 - firebreak
    field = fire_state
    for iteration in range(ITERS):
        first = full_tendency(field, burnable_int, fuel_class, ignition, spread_rate, spread_rows, spread_cols, reaction, ignition_heat)
        middle = field + first
        second = full_tendency(middle, burnable_int, fuel_class, ignition, spread_rate, spread_rows, spread_cols, reaction, ignition_heat)
        field = field + 0.5 * (first + second)
    return field
```

```python
import jax
import jax.numpy as jnp
from jax import lax
from jax.experimental import pallas as pl
from jax.experimental.pallas import tpu as pltpu
from jax.sharding import PartitionSpec as P

ITERS = 4
HALO = 2 * ITERS
C, ROWS, COLS = 64, 48, 128
HALF = ROWS + 2 * HALO
TILES = COLS // 2 + HALO
PLANES = C + 8
GROUP = 24
BF = jnp.bfloat16
F32 = jnp.float32


def split(x):
    hi = x.astype(BF)
    return hi, (x - hi.astype(F32)).astype(BF)


def mirror(x):
    lane = lax.broadcasted_iota(jnp.int32, x.shape, 1)
    idx = jnp.where(lane < 64, lane, 191 - lane)
    return jnp.take_along_axis(x, idx, axis=1)


def turn_kernel(x_ref, m_ref, top_ref, bot_ref, out_ref, left_ref, right_ref):
    flat = out_ref.reshape(64 * PLANES, 128)

    def plane(ch, rows):
        p = jnp.concatenate([top_ref[ch], rows, bot_ref[ch]], axis=0)
        q = mirror(p)
        stacked = jnp.concatenate([q, pltpu.roll(q, 64, 1)], axis=0)
        flat[pl.ds(ch, 64, stride=PLANES), :] = stacked.T[0:64, :]

    def loop(i, _):
        for k in range(8):
            plane(i * 8 + k, x_ref[i * 8 + k])
        return 0

    lax.fori_loop(0, C // 8, loop, 0)
    for k in range(3):
        plane(C + k, m_ref[k])
    for j in range(64):
        out_ref[j, C + 3 :, :] = jnp.zeros((5, 128), F32)
    low = lax.broadcasted_iota(jnp.int32, (PLANES, 128), 1) < 64
    for t in range(4):
        near, far = out_ref[t], pltpu.roll(out_ref[4 + t], 64, 1)
        left_ref[t] = jnp.where(low, near, far)
        right_ref[t] = jnp.where(low, far, near)


def turn(x, masks, top, bot):
    message = jax.ShapeDtypeStruct((4, PLANES, 128), F32)
    return pl.pallas_call(
        turn_kernel,
        name="turn",
        out_shape=(jax.ShapeDtypeStruct((64, PLANES, 128), F32), message, message),
        compiler_params=pltpu.CompilerParams(vmem_limit_bytes=48 * 2**20),
    )(x, masks, top, bot)


def stages_kernel(
    f_ref, left_ref, right_ref, rate_ref, heat_ref, rows_ref, cols_ref, react_ref,
    out_ref, A, B, brate, burn, lit, w_mix, w_react, table,
):
    r_hi, r_lo = split(rows_ref[...])
    c_hi, c_lo = split(cols_ref[...])
    e_hi, e_lo = split(react_ref[...])
    zero = jnp.zeros((64, 64), BF)
    w_mix[0:64, :] = jnp.concatenate([r_hi, c_hi, r_hi, c_hi], 1)
    w_mix[64:128, :] = jnp.concatenate([r_lo, c_lo, zero, zero], 1)
    table[...] = jnp.zeros_like(table)
    table[0:13, 0:64] = rate_ref[...]
    table[13:14, 0:64] = heat_ref[...]
    by_channel = table[...].T[0:64, :]
    t_hi, t_lo = split(by_channel)
    h_hi, h_lo = split(by_channel[:, 13:14])
    lane = lax.broadcasted_iota(jnp.int32, (64, 64), 1)
    heat = jnp.where(lane == 0, h_hi.astype(F32), jnp.where(lane == 1, h_lo.astype(F32), 0.0))
    w_react[...] = jnp.concatenate([e_hi, e_hi, e_lo, heat.astype(BF)], 1)
    w_rate = jnp.concatenate([t_hi, t_lo], 1)

    low = lax.broadcasted_iota(jnp.int32, (PLANES, 128), 1) < 64
    classes = lax.broadcasted_iota(jnp.int32, (128, 128), 0).astype(F32)

    def place(j, tile):
        A[j + 1] = tile[0:C]
        m = tile[C : C + 8]
        burn[j] = jnp.broadcast_to(m[1:2], (8, 128))
        onehot = jnp.where(classes == m[0:1], m[1:2], 0.0).astype(BF)
        brate[j] = jnp.dot(w_rate, jnp.concatenate([onehot, onehot], 0), preferred_element_type=F32)
        lit[j] = jnp.where(classes[0:16] < 2, m[2:3], 0.0).astype(BF)

    for t in range(4):
        from_right, from_left = left_ref[t], right_ref[t]
        place(7 - t, pltpu.roll(jnp.where(low, from_right, from_left), 64, 1))
        place(3 - t, jnp.where(low, from_left, from_right))

    def fill(i, _):
        for k in range(16):
            place(HALO + i * 16 + k, f_ref[i * 16 + k])
        return 0

    lax.fori_loop(0, 4, fill, 0)
    A[0] = jnp.zeros((C, 128), F32)
    B[0] = jnp.zeros((C, 128), F32)
    A[TILES + 1] = pltpu.roll(A[TILES], 64, 1)

    def block(src, dst, b, second):
        xs = [src[b + k] for k in range(GROUP + 2)]
        for p in range(0, GROUP, 2):
            plain, mix, react = [], [], []
            for k in (p, p + 1):
                x = xs[k + 1]
                x2 = x + x
                v = pltpu.roll(x, 1, 1) + pltpu.roll(x, 127, 1) - x2
                h = xs[k] + xs[k + 2] - x2
                v_hi, v_lo = split(v)
                h_hi, h_lo = split(h)
                s_hi, s_lo = split(jnp.tanh(x))
                mix.append(jnp.concatenate([v_hi, h_hi, v_lo, h_lo], 0))
                react.append(jnp.concatenate([s_hi, s_lo, s_hi, lit[b + k], jnp.zeros((48, 128), BF)], 0))
                plain.append(v + h)
            mm = jnp.dot(w_mix[...], jnp.concatenate(mix, 1), preferred_element_type=F32)
            rr = jnp.dot(w_react[...], jnp.concatenate(react, 1), preferred_element_type=F32)
            for i, k in enumerate((p, p + 1)):
                at = slice(128 * i, 128 * i + 128)
                mixed = plain[i] + (mm[0:64, at] + mm[64:128, at])
                drive = brate[b + k] * mixed + burn[b + k][0:1] * rr[:, at]
                if not second:
                    dst[b + k + 1] = 0.5 * xs[k + 1] + drive
                else:
                    dst[b + k + 1] = 0.5 * dst[b + k + 1] + (0.25 * xs[k + 1] + 0.5 * drive)

    def step(s, _):
        def first(i, _):
            block(A, B, i * GROUP, False)
            return 0

        def second(i, _):
            block(B, A, i * GROUP, True)
            return 0

        lax.fori_loop((2 * s + 1) // GROUP, TILES // GROUP, first, 0)
        B[TILES + 1] = pltpu.roll(B[TILES], 64, 1)
        lax.fori_loop((2 * s + 2) // GROUP, TILES // GROUP, second, 0)
        A[TILES + 1] = pltpu.roll(A[TILES], 64, 1)
        return 0

    lax.fori_loop(0, ITERS, step, 0)

    flat = A.reshape((TILES + 2) * C, 128)
    is_low = lax.broadcasted_iota(jnp.int32, (ROWS, 128), 1) < 64

    def back(i, _):
        for k in range(8):
            ch = i * 8 + k
            tiles = flat[pl.ds((HALO + 1) * C + ch, 64, stride=C), :]
            turned = tiles.T
            both = jnp.concatenate([turned[HALO : HALO + ROWS], turned[64 + HALO : 64 + HALO + ROWS]], 1)
            out_ref[ch] = mirror(both)
        return 0

    lax.fori_loop(0, C // 8, back, 0)


def stages(field, left, right, *params):
    return pl.pallas_call(
        stages_kernel,
        name="stages",
        out_shape=jax.ShapeDtypeStruct((C, ROWS, COLS), F32),
        scratch_shapes=[
            pltpu.VMEM((TILES + 2, C, 128), F32),
            pltpu.VMEM((TILES + 2, C, 128), F32),
            pltpu.VMEM((TILES, C, 128), F32),
            pltpu.VMEM((TILES, 8, 128), F32),
            pltpu.VMEM((TILES, 16, 128), BF),
            pltpu.VMEM((128, 256), BF),
            pltpu.VMEM((64, 256), BF),
            pltpu.VMEM((128, 128), F32),
        ],
        compiler_params=pltpu.CompilerParams(vmem_limit_bytes=56 * 2**20),
    )(field, left, right, *params)


def exchange(to_lower, to_upper, axis):
    up = [(i, i + 1) for i in range(lax.axis_size(axis) - 1)]
    down = [(b, a) for a, b in up]
    return lax.ppermute(to_lower, axis, down), lax.ppermute(to_upper, axis, up)


def per_device(
    fire_state, fuel_class, firebreak, ignition,
    spread_rate, spread_rows, spread_cols, reaction, ignition_heat,
):
    masks = jnp.stack([fuel_class, 1 - firebreak, ignition]).astype(F32)
    first = jnp.concatenate([fire_state[:, :HALO], masks[:, :HALO]], 0)
    last = jnp.concatenate([fire_state[:, ROWS - HALO :], masks[:, ROWS - HALO :]], 0)
    bot, top = exchange(first, last, "row")
    field, left, right = turn(fire_state, masks, top, bot)
    from_right, from_left = exchange(left, right, "col")
    return stages(
        field, from_right, from_left,
        spread_rate, ignition_heat[None], spread_rows, spread_cols, reaction,
    )


def solution(mesh):
    whole = P(None, "row", "col")
    cells = P("row", "col")
    return jax.shard_map(
        per_device,
        mesh=mesh,
        in_specs=(whole, cells, cells, cells, P(), P(), P(), P(), P()),
        out_specs=whole,
        check_vma=False,
    )
```

```python
import jax
import jax.numpy as jnp
from jax import lax
from jax.experimental import pallas as pl
from jax.experimental.pallas import tpu as pltpu
from jax.sharding import PartitionSpec as P

ITERS = 4
STAGES = 2 * ITERS
HALO = STAGES
C, ROWS, COLS = 64, 48, 128
HEIGHT = ROWS + 2 * HALO
WIDTH = COLS + 2 * HALO
TILES = HEIGHT // 2
OWN = TILES - HALO
LANES = 2 * C
GROUP = 8
MSG = 4 * WIDTH
BF = jnp.bfloat16
F32 = jnp.float32


def split(x):
    hi = x.astype(BF)
    return hi, (x - hi.astype(F32)).astype(BF)


def lanes(shape):
    return lax.broadcasted_iota(jnp.int32, shape, len(shape) - 1)


def call(kernel, name, outs, scratch=(), limit=12):
    return pl.pallas_call(
        kernel,
        name=name,
        out_shape=[jax.ShapeDtypeStruct(s, d) for s, d in outs],
        scratch_shapes=[pltpu.VMEM(s, d) for s, d in scratch],
        compiler_params=pltpu.CompilerParams(vmem_limit_bytes=limit * 2**20),
    )


FUEL, BURN, LIT = 0, HEIGHT, 2 * HEIGHT


def pack_kernel(x_ref, fuel_ref, break_ref, lit_ref, field_ref, masks_ref, left_ref, right_ref):
    masks_ref[...] = jnp.zeros_like(masks_ref)
    masks_ref[FUEL + HALO : FUEL + HALO + ROWS] = fuel_ref[...].astype(F32)
    masks_ref[BURN + HALO : BURN + HALO + ROWS] = (1 - break_ref[...]).astype(F32)
    masks_ref[LIT + HALO : LIT + HALO + ROWS] = lit_ref[...].astype(F32)
    flat = x_ref.reshape(C * ROWS, COLS)

    def messages(k, turned):
        left_ref[k] = turned[0:HALO]
        right_ref[k] = turned[COLS - HALO :]

    for k in range(OWN):
        top = flat[pl.ds(k, C, stride=ROWS), :]
        bottom = flat[pl.ds(ROWS - 1 - k, C, stride=ROWS), :]
        turned = jnp.concatenate([top, bottom], 0).T
        field_ref[k] = turned
        messages(k, turned)
    messages(OWN, masks_ref[0:128].T)
    messages(OWN + 1, masks_ref[128:256].T)


def pack(x, fuel, firebreak, lit):
    message = ((OWN + 2, HALO, LANES), F32)
    return call(
        pack_kernel, "pack", [((OWN, COLS, LANES), F32), ((256, COLS), F32), message, message]
    )(x, fuel, firebreak, lit)


def onehot(fuel, burn, lit):
    slot = lax.broadcasted_iota(jnp.int32, (C, 128), 0)
    cls = (slot & 15).astype(F32)
    halves = []
    for f, b, i in zip(fuel, burn, lit):
        picked = jnp.where((cls == f) | (cls == 13.0), b, jnp.where(cls == 14.0, b * i, 0.0))
        halves.append(jnp.where(slot < 32, picked, 0.0))
    return jnp.concatenate(halves, 0)


def rates_kernel(
    masks_ref, rate_ref, heat_ref, rows_ref, cols_ref, react_ref,
    brate_ref, burn_ref, bheat_ref, table_ref, w1_ref, w2_ref, w3_ref, tab,
):
    tab[...] = jnp.zeros_like(tab)
    tab[0:13, 0:64] = rate_ref[...]
    tab[14:15, 0:64] = heat_ref[...]
    t = tab[...]
    t = t + pltpu.roll(t, 64, 1)
    row = lax.broadcasted_iota(jnp.int32, (16, 128), 0)
    h = jnp.concatenate(
        [jnp.where(row < 13, t, 0.0), jnp.where(row == 13, 1.0, 0.0), jnp.where(row == 14, t, 0.0)], 1
    )
    hi, lo = split(h)
    half = jnp.concatenate([hi.astype(F32), lo.astype(F32), jnp.zeros((32, 384), F32)], 0)
    low = (lanes((64, 384)) & 127) < 64
    table_ref[...] = jnp.concatenate([jnp.where(low, half, 0.0), jnp.where(low, 0.0, half)], 0).astype(BF)

    zero = jnp.zeros((C, C), F32)
    eye = jnp.where(lax.broadcasted_iota(jnp.int32, (C, C), 0) == lanes((C, C)), 1.0, 0.0)

    def both(m):
        return split(jnp.concatenate([jnp.concatenate([m, zero], 1), jnp.concatenate([zero, m], 1)], 0).T)

    r_hi, r_lo = both(rows_ref[...] + eye)
    c_hi, c_lo = both(cols_ref[...] + eye)
    e_hi, e_lo = both(react_ref[...])
    w1_ref[...] = jnp.concatenate([jnp.concatenate([r_hi, c_hi], 1)] * 2, 0)
    w2_ref[...] = jnp.concatenate([r_lo, c_lo], 1)
    w3_ref[...] = jnp.concatenate(
        [jnp.concatenate([e_hi, e_lo], 1), jnp.concatenate([e_hi, jnp.zeros((128, 128), BF)], 1)], 0
    )
    for r in range(HALO, TILES):
        put_rates(masks_ref, table_ref, r, brate_ref, burn_ref, bheat_ref)


def put_rates(masks_ref, table_ref, r, brate_ref, burn_ref, bheat_ref):
    pick = lambda base: (masks_ref[base + r : base + r + 1], masks_ref[base + 63 - r : base + 64 - r])
    hot = onehot(pick(FUEL), pick(BURN), pick(LIT)).T.astype(BF)
    got = jnp.dot(hot, table_ref[...], preferred_element_type=F32)
    at = slice(HALO, HALO + COLS)
    brate_ref[r, at], burn_ref[r, at], bheat_ref[r, at] = got[:, 0:128], got[:, 128:256], got[:, 256:384]


def put_edge_rates(edge_ref, table_ref, r0, brate_ref, burn_ref, bheat_ref):
    rows = []
    for base in (FUEL, BURN, LIT):
        halves = []
        for h in range(2):
            total = None
            for k in range(8):
                p = r0 + k if h == 0 else 63 - r0 - k
                part = edge_ref[base + p : base + p + 1]
                part = pltpu.roll(part, 16 * k, 1) if k else part
                total = part if total is None else total + part
            halves.append(total)
        rows.append(halves)
    got = jnp.dot(onehot(*rows).T.astype(BF), table_ref[...], preferred_element_type=F32)
    for k in range(8):
        for side, at in ((0, slice(0, HALO)), (8, slice(HALO + COLS, WIDTH))):
            part = got[16 * k + side : 16 * k + side + 8]
            r = r0 + k
            brate_ref[r, at], burn_ref[r, at], bheat_ref[r, at] = part[:, 0:128], part[:, 128:256], part[:, 256:384]


def rates(masks, rate, heat, rows, cols, react):
    cells = ((TILES, WIDTH, LANES), F32)
    return call(
        rates_kernel, "rates",
        [cells, cells, cells, ((128, 384), BF), ((256, 256), BF), ((128, 256), BF), ((256, 256), BF)],
        [((16, 128), F32)],
    )(masks, rate, heat, rows, cols, react)


def turned_edges(left_ref, right_ref, k):
    both = jnp.concatenate([left_ref[k], right_ref[k], jnp.zeros((112, 128), F32)], 0)
    return both.T


def rows_kernel(field_ref, masks_ref, left_ref, right_ref, up_ref, down_ref, edge_ref):
    low = lanes((WIDTH, LANES)) < C

    def tile(k):
        return jnp.concatenate([left_ref[k], field_ref[k], right_ref[k]], 0)

    for t in range(4):
        near, far = tile(t), pltpu.roll(tile(4 + t), C, 1)
        at = slice(t * WIDTH, (t + 1) * WIDTH)
        up_ref[at] = jnp.where(low, near, far)
        down_ref[at] = jnp.where(low, far, near)
    edge_ref[0:128] = turned_edges(left_ref, right_ref, OWN)
    edge_ref[128:256] = turned_edges(left_ref, right_ref, OWN + 1)
    for i, base in enumerate((FUEL, BURN, LIT)):
        for ref, first in ((up_ref, HALO), (down_ref, HALO + ROWS - 8)):
            rows = slice(base + first, base + first + 8)
            ref[MSG + 8 * i : MSG + 8 * i + 8] = masks_ref[rows]
            ref[MSG + 24 + 8 * i : MSG + 32 + 8 * i] = edge_ref[rows]


def row_messages(field, masks, left, right):
    message = ((MSG + 48, LANES), F32)
    return call(rows_kernel, "rows", [message, message, ((256, LANES), F32)])(field, masks, left, right)


def sweep(src, dst, base, first, last, second, rate_of, weights, S, W, T):
    w1, w2, w3 = weights
    brate, burn, bheat = rate_of

    def mix(r, n):
        x = src[r - base : r - base + n].reshape(n * WIDTH, LANES)
        hi, lo = split(x)
        t_hi, t_lo = split(jnp.tanh(x))
        sw = jnp.dot(jnp.concatenate([hi, lo], 1), w1[...], preferred_element_type=F32)
        sw = sw + jnp.dot(hi, w2[...], preferred_element_type=F32)
        tt = jnp.dot(jnp.concatenate([t_hi, t_lo], 1), w3[...], preferred_element_type=F32)
        tt = tt[:, 0:LANES] + tt[:, LANES:]
        for k in range(n):
            at = slice(k * WIDTH, (k + 1) * WIDTH)
            q = r + k
            S[q - base] = sw[at, 0:LANES]
            W[q - base, 8 : 8 + WIDTH] = sw[at, LANES:]
            if first <= q < last:
                T[q - base] = 0.5 * x[at] + (burn(q) * tt[at] + bheat(q))
            if q == TILES - 1:
                S[q - base + 1] = pltpu.roll(sw[at, 0:LANES], C, 1)

    def post(r):
        q = r - base
        centre = S[q] + W[q, 8 : 8 + WIDTH]
        around = (S[q - 1] + S[q + 1]) + (W[q, 7 : 7 + WIDTH] + W[q, 9 : 9 + WIDTH])
        g = T[q] + brate(r) * (around - centre - centre)
        dst[q] = 0.5 * (dst[q] + g) if second else g

    end = min(last + 1, TILES)
    r, todo = first - 1, first
    while r < end:
        n = min(GROUP, end - r)
        if 0 < end - r - n < 3:
            n = end - r
        mix(r, n)
        r += n
        limit = last if r == end else min(last, r - 1)
        for q in range(todo, limit):
            post(q)
        todo = max(todo, limit)


def inner_kernel(
    field_ref, left_ref, right_ref, edge_ref, brate_in, burn_in, bheat_in, table_ref, w1, w2, w3,
    A, B, brate, burn, bheat, S, W, T,
):
    for k in range(OWN):
        A[HALO + k, 0:HALO] = left_ref[k]
        A[HALO + k, HALO : HALO + COLS] = field_ref[k]
        A[HALO + k, HALO + COLS :] = right_ref[k]
    W[...] = jnp.zeros_like(W)
    at = slice(HALO, HALO + COLS)
    for r in range(HALO, TILES):
        brate[r, at], burn[r, at], bheat[r, at] = brate_in[r, at], burn_in[r, at], bheat_in[r, at]
    for r0 in range(HALO, TILES, 8):
        put_edge_rates(edge_ref, table_ref, r0, brate, burn, bheat)
    rate_of = [lambda r, ref=ref: ref[r] for ref in (brate, burn, bheat)]
    for s in range(1, STAGES + 1):
        src, dst = (A, B) if s % 2 else (B, A)
        sweep(src, dst, 0, HALO + s, TILES, s % 2 == 0, rate_of, (w1, w2, w3), S, W, T)


def inner(field, left, right, edge, rate_arrays):
    cells = ((TILES, WIDTH, LANES), F32)
    return call(
        inner_kernel, "inner", [cells] * 5,
        [((TILES + 1, WIDTH, LANES), F32), ((TILES, WIDTH + 16, LANES), F32), ((TILES, WIDTH, LANES), F32)],
    )(field, left, right, edge, *rate_arrays)


def outer_kernel(
    A_in, B_in, brate_in, burn_in, bheat_in, top_ref, bottom_ref, table_ref, w1, w2, w3,
    out_ref, A, B, brate, burn, bheat, masks, edge, S, W, T,
):
    low = lanes((WIDTH, LANES)) < C
    for t in range(4):
        at = slice(t * WIDTH, (t + 1) * WIDTH)
        A[7 - t] = pltpu.roll(jnp.where(low, bottom_ref[at], top_ref[at]), C, 1)
        A[3 - t] = jnp.where(low, top_ref[at], bottom_ref[at])
    for r in range(7, 18):
        if r > 7:
            A[r] = A_in[r]
        B[r] = B_in[r]
    W[...] = jnp.zeros_like(W)
    for i, base in enumerate((FUEL, BURN, LIT)):
        for ref, first in ((top_ref, 0), (bottom_ref, HALO + ROWS)):
            rows = slice(base + first, base + first + 8)
            masks[rows] = ref[MSG + 8 * i : MSG + 8 * i + 8]
            edge[rows] = ref[MSG + 24 + 8 * i : MSG + 32 + 8 * i]
    for r in range(HALO):
        put_rates(masks, table_ref, r, brate, burn, bheat)
    put_edge_rates(edge, table_ref, 0, brate, burn, bheat)
    rate_of = [
        lambda r, near=near, far=far: near[r] if r < HALO else far[r]
        for near, far in ((brate, brate_in), (burn, burn_in), (bheat, bheat_in))
    ]
    for s in range(1, STAGES + 1):
        src, dst = (A, B) if s % 2 else (B, A)
        sweep(src, dst, 0, s, HALO + s, s % 2 == 0, rate_of, (w1, w2, w3), S, W, T)
    flat = out_ref.reshape(C * ROWS, COLS)
    for k in range(OWN):
        r = HALO + k
        turned = (A if r < 2 * HALO else A_in)[r, HALO : HALO + COLS].T
        flat[pl.ds(k, C, stride=ROWS), :] = turned[0:C]
        flat[pl.ds(ROWS - 1 - k, C, stride=ROWS), :] = turned[C:]


def outer(A, B, brate, burn, bheat, top, bottom, weights):
    few = 18
    cells = ((few, WIDTH, LANES), F32)
    edge_cells = ((HALO, WIDTH, LANES), F32)
    return call(
        outer_kernel, "outer", [((C, ROWS, COLS), F32)],
        [cells, cells, edge_cells, edge_cells, edge_cells, ((192, COLS), F32), ((192, COLS), F32),
         cells, ((few, WIDTH + 16, LANES), F32), cells],
    )(A, B, brate, burn, bheat, top, bottom, *weights)[0]


def exchange(to_lower, to_upper, axis):
    up = [(i, i + 1) for i in range(lax.axis_size(axis) - 1)]
    down = [(b, a) for a, b in up]
    return lax.ppermute(to_lower, axis, down), lax.ppermute(to_upper, axis, up)


def per_device(
    fire_state, fuel_class, firebreak, ignition,
    spread_rate, spread_rows, spread_cols, reaction, ignition_heat,
):
    field, masks, first, last = pack(fire_state, fuel_class, firebreak, ignition)
    right, left = exchange(first, last, "col")
    rate_arrays = rates(masks, spread_rate, ignition_heat[None], spread_rows, spread_cols, reaction)
    up, down, edge = row_messages(field, masks, left, right)
    bottom, top = exchange(up, down, "row")
    A, B, brate, burn, bheat = inner(field, left, right, edge, rate_arrays)
    return outer(A, B, brate, burn, bheat, top, bottom, rate_arrays[3:])


def solution(mesh):
    whole = P(None, "row", "col")
    cells = P("row", "col")
    return jax.shard_map(
        per_device,
        mesh=mesh,
        in_specs=(whole, cells, cells, cells, P(), P(), P(), P(), P()),
        out_specs=whole,
        check_vma=False,
    )
```

```python
import jax
import jax.numpy as jnp
from jax import lax
from jax.experimental import pallas as pl
from jax.experimental.pallas import tpu as pltpu
from jax.sharding import PartitionSpec as P

ITERS = 4
STAGES = 2 * ITERS
HALO = STAGES
C, ROWS, COLS = 64, 48, 128
HEIGHT = ROWS + 2 * HALO
WIDTH = COLS + 2 * HALO
TILES = HEIGHT // 2
OWN = TILES - HALO
LANES = 2 * C
INNER_GROUP = 8
OUTER_GROUP = 4
MSG = 4 * WIDTH
BF = jnp.bfloat16
F32 = jnp.float32


def split(x):
    hi = x.astype(BF)
    return hi, (x - hi.astype(F32)).astype(BF)


def lanes(shape):
    return lax.broadcasted_iota(jnp.int32, shape, len(shape) - 1)


def call(kernel, name, outs, scratch=(), limit=12, from_hbm=0, extra=()):
    specs = {"in_specs": [pl.BlockSpec(memory_space=pltpu.HBM)] * from_hbm} if from_hbm else {}
    return pl.pallas_call(
        kernel,
        name=name,
        out_shape=[jax.ShapeDtypeStruct(s, d) for s, d in outs],
        scratch_shapes=[pltpu.VMEM(s, d) for s, d in scratch] + list(extra),
        **specs,
        compiler_params=pltpu.CompilerParams(vmem_limit_bytes=limit * 2**20),
    )


FUEL, BURN, LIT = 0, HEIGHT, 2 * HEIGHT


def even(axis):
    return lax.rem(lax.axis_index(axis), 2) == 0


def pack_kernel(
    x_hbm, fuel_hbm, break_hbm, lit_hbm, field_ref, masks_ref, near_ref, far_ref, x_ref, ints, sems
):
    copies = [
        pltpu.make_async_copy(x_hbm.at[:, pl.ds(8 * g, 8), :], x_ref.at[:, pl.ds(8 * g, 8), :], sems.at[g])
        for g in range(ROWS // 8)
    ]
    for g in (0, 5, 1, 4, 2, 3):
        copies[g].start()
    small = [
        pltpu.make_async_copy(ref, ints.at[i], sems.at[6 + i])
        for i, ref in enumerate((fuel_hbm, break_hbm, lit_hbm))
    ]
    for copy in small:
        copy.start()
    masks_ref[...] = jnp.zeros_like(masks_ref)
    flat = x_ref.reshape(C * ROWS, COLS)
    is_even = even("col")

    def messages(k, turned):
        first, last = turned[0:HALO], turned[COLS - HALO :]
        near_ref[k] = jnp.where(is_even, last, first)
        far_ref[k] = jnp.where(is_even, first, last)

    for k in range(OWN):
        if k % 8 == 0:
            copies[k // 8].wait()
            copies[5 - k // 8].wait()
        top = flat[pl.ds(k, C, stride=ROWS), :]
        bottom = flat[pl.ds(ROWS - 1 - k, C, stride=ROWS), :]
        turned = jnp.concatenate([top, bottom], 0).T
        field_ref[k] = turned
        messages(k, turned)
    for copy in small:
        copy.wait()
    masks_ref[FUEL + HALO : FUEL + HALO + ROWS] = ints[0].astype(F32)
    masks_ref[BURN + HALO : BURN + HALO + ROWS] = (1 - ints[1]).astype(F32)
    masks_ref[LIT + HALO : LIT + HALO + ROWS] = ints[2].astype(F32)
    messages(OWN, masks_ref[0:128].T)
    messages(OWN + 1, masks_ref[128:256].T)


def pack(x, fuel, firebreak, lit):
    message = ((OWN + 2, HALO, LANES), F32)
    return call(
        pack_kernel, "pack", [((OWN, COLS, LANES), F32), ((256, COLS), F32), message, message],
        [((C, ROWS, COLS), F32)], from_hbm=4,
        extra=[pltpu.VMEM((3, ROWS, COLS), jnp.int32), pltpu.SemaphoreType.DMA((9,))],
    )(x, fuel, firebreak, lit)


def onehot(fuel, burn, lit):
    slot = lax.broadcasted_iota(jnp.int32, (C, 128), 0)
    cls = (slot & 15).astype(F32)
    halves = []
    for f, b, i in zip(fuel, burn, lit):
        picked = jnp.where((cls == f) | (cls == 13.0), b, jnp.where(cls == 14.0, b * i, 0.0))
        halves.append(jnp.where(slot < 32, picked, 0.0))
    return jnp.concatenate(halves, 0)


def rates_kernel(
    masks_ref, rate_ref, heat_ref, rows_ref, cols_ref, react_ref,
    brate_ref, burn_ref, bheat_ref, table_ref, w1_ref, w2_ref, w3_ref, tab,
):
    tab[...] = jnp.zeros_like(tab)
    tab[0:13, 0:64] = rate_ref[...]
    tab[14:15, 0:64] = heat_ref[...]
    t = tab[...]
    t = t + pltpu.roll(t, 64, 1)
    row = lax.broadcasted_iota(jnp.int32, (16, 128), 0)
    h = jnp.concatenate(
        [jnp.where(row < 13, t, 0.0), jnp.where(row == 13, 1.0, 0.0), jnp.where(row == 14, t, 0.0)], 1
    )
    hi, lo = split(h)
    half = jnp.concatenate([hi.astype(F32), lo.astype(F32), jnp.zeros((32, 384), F32)], 0)
    low = (lanes((64, 384)) & 127) < 64
    table_ref[...] = jnp.concatenate([jnp.where(low, half, 0.0), jnp.where(low, 0.0, half)], 0).astype(BF)

    zero = jnp.zeros((C, C), F32)
    eye = jnp.where(lax.broadcasted_iota(jnp.int32, (C, C), 0) == lanes((C, C)), 1.0, 0.0)

    def both(m):
        return split(jnp.concatenate([jnp.concatenate([m, zero], 1), jnp.concatenate([zero, m], 1)], 0).T)

    r_hi, r_lo = both(rows_ref[...] + eye)
    c_hi, c_lo = both(cols_ref[...] + eye)
    e_hi, e_lo = both(react_ref[...])
    w1_ref[...] = jnp.concatenate([jnp.concatenate([r_hi, c_hi], 1)] * 2, 0)
    w2_ref[...] = jnp.concatenate([r_lo, c_lo], 1)
    w3_ref[...] = jnp.concatenate(
        [jnp.concatenate([e_hi, e_lo], 1), jnp.concatenate([e_hi, jnp.zeros((128, 128), BF)], 1)], 0
    )
    for k in range(OWN):
        put_rates(masks_ref, table_ref, HALO + k, k, 0, brate_ref, burn_ref, bheat_ref)


def put_rates(masks_ref, table_ref, r, k, start, brate_ref, burn_ref, bheat_ref):
    pick = lambda base: (masks_ref[base + r : base + r + 1], masks_ref[base + 63 - r : base + 64 - r])
    hot = onehot(pick(FUEL), pick(BURN), pick(LIT)).T.astype(BF)
    got = jnp.dot(hot, table_ref[...], preferred_element_type=F32)
    at = slice(start, start + COLS)
    brate_ref[k, at], burn_ref[k, at], bheat_ref[k, at] = got[:, 0:128], got[:, 128:256], got[:, 256:384]


def put_edge_rates(edge_ref, table_ref, r0, base_r, starts, brate_ref, burn_ref, bheat_ref):
    rows = []
    for base in (FUEL, BURN, LIT):
        halves = []
        for h in range(2):
            total = None
            for k in range(8):
                p = r0 + k if h == 0 else 63 - r0 - k
                part = edge_ref[base + p : base + p + 1]
                part = pltpu.roll(part, 16 * k, 1) if k else part
                total = part if total is None else total + part
            halves.append(total)
        rows.append(halves)
    got = jnp.dot(onehot(*rows).T.astype(BF), table_ref[...], preferred_element_type=F32)
    for k in range(8):
        for side, start in zip((0, 8), starts):
            part = got[16 * k + side : 16 * k + side + 8]
            r, at = r0 + k - base_r, slice(start, start + HALO)
            brate_ref[r, at], burn_ref[r, at], bheat_ref[r, at] = part[:, 0:128], part[:, 128:256], part[:, 256:384]


def rates(masks, rate, heat, rows, cols, react):
    cells = ((OWN, COLS, LANES), F32)
    return call(
        rates_kernel, "rates",
        [cells, cells, cells, ((128, 384), BF), ((256, 256), BF), ((128, 256), BF), ((256, 256), BF)],
        [((16, 128), F32)],
    )(masks, rate, heat, rows, cols, react)


def turned_edges(left_ref, right_ref, k):
    both = jnp.concatenate([left_ref[k], right_ref[k], jnp.zeros((112, 128), F32)], 0)
    return both.T


def rows_kernel(
    field_ref, masks_ref, near_ref, far_ref, table_ref,
    out_near_ref, out_far_ref, edge_ref, left_ref, right_ref, up_ref, down_ref,
):
    is_even = even("col")
    left_ref[...] = jnp.where(is_even, far_ref[...], near_ref[...])
    right_ref[...] = jnp.where(is_even, near_ref[...], far_ref[...])
    low = lanes((WIDTH, LANES)) < C

    def tile(k):
        return jnp.concatenate([left_ref[k], field_ref[k], right_ref[k]], 0)

    for t in range(4):
        near, far = tile(t), pltpu.roll(tile(4 + t), C, 1)
        at = slice(t * WIDTH, (t + 1) * WIDTH)
        up_ref[at] = jnp.where(low, near, far)
        down_ref[at] = jnp.where(low, far, near)
    edge_ref[0:128] = turned_edges(left_ref, right_ref, OWN)
    edge_ref[128:256] = turned_edges(left_ref, right_ref, OWN + 1)
    for i, base in enumerate((FUEL, BURN, LIT)):
        for ref, first in ((up_ref, HALO), (down_ref, HALO + ROWS - 8)):
            rows = slice(base + first, base + first + 8)
            ref[MSG + 8 * i : MSG + 8 * i + 8] = masks_ref[rows]
            ref[MSG + 24 + 8 * i : MSG + 32 + 8 * i] = edge_ref[rows]
    row_even = even("row")
    out_near_ref[...] = jnp.where(row_even, down_ref[...], up_ref[...])
    out_far_ref[...] = jnp.where(row_even, up_ref[...], down_ref[...])


def row_messages(field, masks, near, far, table):
    message = ((MSG + 48, LANES), F32)
    side = ((OWN + 2, HALO, LANES), F32)
    return call(
        rows_kernel, "rows", [message, message, ((256, LANES), F32), side, side], [message, message]
    )(field, masks, near, far, table)


class Stage:
    def __init__(self, first, last, second, load, old, store, rate, weights, S, W, T, group):
        self.first, self.last, self.second = first, last, second
        self.load, self.old, self.store, self.rate = load, old, store, rate
        self.weights, self.S, self.W, self.T, self.group = weights, S, W, T, group

    def mix(self, r, n, keep=None):
        w1, w2, w3 = self.weights
        brate, burn, bheat = self.rate
        x = jnp.concatenate([self.load(r + k) for k in range(n)], 0)
        hi, lo = split(x)
        t_hi, t_lo = split(jnp.tanh(x))
        sw = jnp.dot(jnp.concatenate([hi, lo], 1), w1[...], preferred_element_type=F32)
        sw = sw + jnp.dot(hi, w2[...], preferred_element_type=F32)
        tt = jnp.dot(jnp.concatenate([t_hi, t_lo], 1), w3[...], preferred_element_type=F32)
        tt = tt[:, 0:LANES] + tt[:, LANES:]
        for k in range(n):
            at = slice(k * WIDTH, (k + 1) * WIDTH)
            q = r + k
            rest = None
            self.S[q] = sw[at, 0:LANES]
            self.W[q, 8 : 8 + WIDTH] = sw[at, LANES:]
            if self.first <= q < self.last or keep:
                rest = 0.5 * x[at] + (burn(q) * tt[at] + bheat(q))
                self.T[q] = rest
            if q == TILES - 1:
                self.S[q + 1] = pltpu.roll(sw[at, 0:LANES], C, 1)
            if keep:
                keep(q, sw[at, 0:LANES], sw[at, LANES:], rest)

    def post(self, q, s_at, w_at, t_at):
        centre = s_at(q) + w_at(q, 8)
        around = (s_at(q - 1) + s_at(q + 1)) + (w_at(q, 7) + w_at(q, 9))
        g = t_at(q) + self.rate[0](q) * (around - centre - centre)
        self.store(q, 0.5 * (self.old(q) + g) if self.second else g)

    def run(self, end, s_at, w_at, t_at, keep=None):
        r, todo = self.first - 1, self.first
        while r < end:
            n = min(self.group, end - r)
            if 0 < end - r - n < 3:
                n = end - r
            self.mix(r, n, keep)
            r += n
            limit = self.last if r == end else min(self.last, r - 1)
            for q in range(todo, limit):
                self.post(q, s_at, w_at, t_at)
            todo = max(todo, limit)


def beside(side, own):
    return lambda r: jnp.concatenate([side[r - HALO, 0:8], own[r - HALO], side[r - HALO, 8:16]], 0)


def clear_margins(W):
    W[:, 0:8] = jnp.zeros((W.shape[0], 8, LANES), F32)
    W[:, 8 + WIDTH :] = jnp.zeros((W.shape[0], 8, LANES), F32)


def inner_kernel(
    field_ref, left_ref, right_ref, edge_ref, brate_in, burn_in, bheat_in, table_ref, w1, w2, w3,
    A, B, brate, burn, bheat, kept_s, kept_w, kept_t, S, W, T,
):
    clear_margins(W)
    clear_margins(kept_w)
    for r0 in range(HALO, TILES, 8):
        put_edge_rates(edge_ref, table_ref, r0, HALO, (0, 8), brate, burn, bheat)
    rate = [beside(brate, brate_in), beside(burn, burn_in), beside(bheat, bheat_in)]

    def start(r):
        k = r - HALO
        return jnp.concatenate([left_ref[k], field_ref[k], right_ref[k]], 0)

    A[HALO] = start(HALO)
    A[HALO + 1] = start(HALO + 1)
    for s in range(1, STAGES + 1):
        src, dst = (A, B) if s % 2 else (B, A)

        def store(q, value, dst=dst):
            dst[q] = value

        def keep(q, s_value, w_value, t_value, s=s):
            near = q - (HALO + s - 1)
            if near < 2:
                kept_s[s - 1, near] = s_value
            if near == 0:
                kept_w[s - 1, 8 : 8 + WIDTH] = w_value
                kept_t[s - 1] = t_value

        stage = Stage(
            HALO + s, TILES, s % 2 == 0,
            start if s == 1 else (lambda r, src=src: src[r]),
            start if s == 2 else (lambda r, dst=dst: dst[r]),
            store, rate, (w1, w2, w3), S, W, T, INNER_GROUP,
        )
        stage.run(TILES, lambda q: S[q], lambda q, o: W[q, o : o + WIDTH], lambda q: T[q], keep)


def inner(field, left, right, edge, rate_arrays):
    cells = ((TILES, WIDTH, LANES), F32)
    edges = ((OWN, 2 * HALO, LANES), F32)
    return call(
        inner_kernel, "inner",
        [cells, cells, edges, edges, edges, ((STAGES, 2, WIDTH, LANES), F32),
         ((STAGES, WIDTH + 16, LANES), F32), ((STAGES, WIDTH, LANES), F32)],
        [((TILES + 1, WIDTH, LANES), F32), ((TILES, WIDTH + 16, LANES), F32), cells],
    )(field, left, right, edge, *rate_arrays)


def outer_kernel(
    A_in, B_in, brate_side, burn_side, bheat_side, kept_s, kept_w, kept_t, brate_in, burn_in, bheat_in,
    near_ref, far_ref, table_ref, w1, w2, w3,
    out_ref, A, B, brate, burn, bheat, masks, edge, S, W, T,
):
    low = lanes((WIDTH, LANES)) < C
    row_even = even("row")

    def arrived(at):
        near, far = near_ref[at], far_ref[at]
        return jnp.where(row_even, far, near), jnp.where(row_even, near, far)

    for t in range(4):
        top, bottom = arrived(slice(t * WIDTH, (t + 1) * WIDTH))
        A[7 - t] = pltpu.roll(jnp.where(low, bottom, top), C, 1)
        A[3 - t] = jnp.where(low, top, bottom)
    clear_margins(W)
    for i, base in enumerate((FUEL, BURN, LIT)):
        for ref, offset in ((masks, MSG + 8 * i), (edge, MSG + 24 + 8 * i)):
            top, bottom = arrived(slice(offset, offset + 8))
            ref[base : base + 8] = top
            ref[base + HALO + ROWS : base + HEIGHT] = bottom
    for r in range(HALO):
        put_rates(masks, table_ref, r, r, HALO, brate, burn, bheat)
    put_edge_rates(edge, table_ref, 0, 0, (0, HALO + COLS), brate, burn, bheat)

    def reader(near, side, own):
        far = beside(side, own)
        return lambda r: near[r] if r < HALO else far(r)

    rate = [
        reader(brate, brate_side, brate_in), reader(burn, burn_side, burn_in), reader(bheat, bheat_side, bheat_in)
    ]
    for s in range(1, STAGES + 1):
        (src, dst), dst_in = ((A, B), B_in) if s % 2 else ((B, A), A_in)
        edge_tile = HALO + s - 1

        def store(q, value, dst=dst):
            dst[q] = value

        def old(q, dst=dst, dst_in=dst_in, s=s):
            return dst[q] if q < HALO + s - 2 else dst_in[q]

        def load(q, src=src):
            return src[q]

        def s_at(q, e=edge_tile, s=s):
            return S[q] if q < e else kept_s[s - 1, q - e]

        def w_at(q, o, e=edge_tile, s=s):
            return W[q, o : o + WIDTH] if q < e else kept_w[s - 1, o : o + WIDTH]

        def t_at(q, e=edge_tile, s=s):
            return T[q] if q < e else kept_t[s - 1]

        stage = Stage(
            s, HALO + s, s % 2 == 0, load, old, store, rate, (w1, w2, w3), S, W, T, OUTER_GROUP
        )
        stage.run(edge_tile, s_at, w_at, t_at)
    flat = out_ref.reshape(C * ROWS, COLS)
    for k in reversed(range(OWN)):
        r = HALO + k
        turned = (A if r < 2 * HALO else A_in)[r, HALO : HALO + COLS].T
        flat[pl.ds(k, C, stride=ROWS), :] = turned[0:C]
        flat[pl.ds(ROWS - 1 - k, C, stride=ROWS), :] = turned[C:]


def outer(states, rate_arrays, near, far):
    few = 2 * HALO
    cells = ((few, WIDTH, LANES), F32)
    edge_cells = ((HALO, WIDTH, LANES), F32)
    return call(
        outer_kernel, "outer", [((C, ROWS, COLS), F32)],
        [cells, cells, edge_cells, edge_cells, edge_cells, ((192, COLS), F32), ((192, COLS), F32),
         cells, ((few, WIDTH + 16, LANES), F32), cells],
    )(*states, *rate_arrays[:3], near, far, *rate_arrays[3:])[0]


def exchange(near, far, axis):
    size = lax.axis_size(axis)

    def swap(x, start):
        pairs = [(i, i + 1) for i in range(start, size - 1, 2)]
        return lax.ppermute(x, axis, pairs + [(b, a) for a, b in pairs])

    far = swap(far, 1)
    return swap(near, 0), far


def per_device(
    fire_state, fuel_class, firebreak, ignition,
    spread_rate, spread_rows, spread_cols, reaction, ignition_heat,
):
    field, masks, near, far = pack(fire_state, fuel_class, firebreak, ignition)
    near, far = exchange(near, far, "col")
    rate_arrays = rates(masks, spread_rate, ignition_heat[None], spread_rows, spread_cols, reaction)
    near, far, edge, left, right = row_messages(field, masks, near, far, rate_arrays[3])
    near, far = exchange(near, far, "row")
    states = inner(field, left, right, edge, rate_arrays)
    return outer(states, rate_arrays, near, far)


def solution(mesh):
    whole = P(None, "row", "col")
    cells = P("row", "col")
    return jax.shard_map(
        per_device,
        mesh=mesh,
        in_specs=(whole, cells, cells, cells, P(), P(), P(), P(), P()),
        out_specs=whole,
        check_vma=False,
    )
```

```python
import jax
import jax.numpy as jnp
from jax import lax
from jax.experimental import pallas as pl
from jax.experimental.pallas import tpu as pltpu
from jax.sharding import PartitionSpec as P

ITERS = 4
STAGES = 2 * ITERS
HALO = STAGES
C, ROWS, COLS = 64, 48, 128
HEIGHT = ROWS + 2 * HALO
WIDTH = COLS + 2 * HALO
TILES = HEIGHT // 2
OWN = TILES - HALO
LANES = 2 * C
INNER_GROUP = 8
OUTER_GROUP = 4
MSG = 4 * WIDTH
BF = jnp.bfloat16
F32 = jnp.float32


def split(x):
    hi = x.astype(BF)
    return hi, (x - hi.astype(F32)).astype(BF)


def lanes(shape):
    return lax.broadcasted_iota(jnp.int32, shape, len(shape) - 1)


def call(kernel, name, outs, scratch=(), limit=12, from_hbm=0, extra=()):
    specs = {"in_specs": [pl.BlockSpec(memory_space=pltpu.HBM)] * from_hbm} if from_hbm else {}
    return pl.pallas_call(
        kernel,
        name=name,
        out_shape=[jax.ShapeDtypeStruct(s, d) for s, d in outs],
        scratch_shapes=[pltpu.VMEM(s, d) for s, d in scratch] + list(extra),
        **specs,
        compiler_params=pltpu.CompilerParams(vmem_limit_bytes=limit * 2**20),
    )


FUEL, BURN, LIT = 0, HEIGHT, 2 * HEIGHT


def even(axis):
    return lax.rem(lax.axis_index(axis), 2) == 0


def pack_kernel(
    x_hbm, fuel_hbm, break_hbm, lit_hbm, field_ref, masks_ref, near_ref, far_ref, x_ref, ints, sems
):
    copies = [
        pltpu.make_async_copy(x_hbm.at[:, pl.ds(8 * g, 8), :], x_ref.at[:, pl.ds(8 * g, 8), :], sems.at[g])
        for g in range(ROWS // 8)
    ]
    for g in (0, 5, 1, 4, 2, 3):
        copies[g].start()
    small = [
        pltpu.make_async_copy(ref, ints.at[i], sems.at[6 + i])
        for i, ref in enumerate((fuel_hbm, break_hbm, lit_hbm))
    ]
    for copy in small:
        copy.start()
    masks_ref[...] = jnp.zeros_like(masks_ref)
    flat = x_ref.reshape(C * ROWS, COLS)
    is_even = even("col")

    def messages(k, turned):
        first, last = turned[0:HALO], turned[COLS - HALO :]
        near_ref[k] = jnp.where(is_even, last, first)
        far_ref[k] = jnp.where(is_even, first, last)

    for k in range(OWN):
        if k % 8 == 0:
            copies[k // 8].wait()
            copies[5 - k // 8].wait()
        top = flat[pl.ds(k, C, stride=ROWS), :]
        bottom = flat[pl.ds(ROWS - 1 - k, C, stride=ROWS), :]
        turned = jnp.concatenate([top, bottom], 0).T
        field_ref[k] = turned
        messages(k, turned)
    for copy in small:
        copy.wait()
    masks_ref[FUEL + HALO : FUEL + HALO + ROWS] = ints[0].astype(F32)
    masks_ref[BURN + HALO : BURN + HALO + ROWS] = (1 - ints[1]).astype(F32)
    masks_ref[LIT + HALO : LIT + HALO + ROWS] = ints[2].astype(F32)
    messages(OWN, masks_ref[0:128].T)
    messages(OWN + 1, masks_ref[128:256].T)


def pack(x, fuel, firebreak, lit):
    message = ((OWN + 2, HALO, LANES), F32)
    return call(
        pack_kernel, "pack", [((OWN, COLS, LANES), F32), ((256, COLS), F32), message, message],
        [((C, ROWS, COLS), F32)], from_hbm=4,
        extra=[pltpu.VMEM((3, ROWS, COLS), jnp.int32), pltpu.SemaphoreType.DMA((9,))],
    )(*[pltpu.with_memory_space_constraint(a, pltpu.HBM) for a in (x, fuel, firebreak, lit)])


def onehot(fuel, burn, lit):
    slot = lax.broadcasted_iota(jnp.int32, (C, 128), 0)
    cls = (slot & 15).astype(F32)
    halves = []
    for f, b, i in zip(fuel, burn, lit):
        picked = jnp.where((cls == f) | (cls == 13.0), b, jnp.where(cls == 14.0, b * i, 0.0))
        halves.append(jnp.where(slot < 32, picked, 0.0))
    return jnp.concatenate(halves, 0)


def rates_kernel(
    masks_ref, rate_ref, heat_ref, rows_ref, cols_ref, react_ref,
    brate_ref, burn_ref, bheat_ref, table_ref, w1_ref, w2_ref, w3_ref, tab,
):
    tab[...] = jnp.zeros_like(tab)
    tab[0:13, 0:64] = rate_ref[...]
    tab[14:15, 0:64] = heat_ref[...]
    t = tab[...]
    t = t + pltpu.roll(t, 64, 1)
    row = lax.broadcasted_iota(jnp.int32, (16, 128), 0)
    h = jnp.concatenate(
        [jnp.where(row < 13, t, 0.0), jnp.where(row == 13, 1.0, 0.0), jnp.where(row == 14, t, 0.0)], 1
    )
    hi, lo = split(h)
    half = jnp.concatenate([hi.astype(F32), lo.astype(F32), jnp.zeros((32, 384), F32)], 0)
    low = (lanes((64, 384)) & 127) < 64
    table_ref[...] = jnp.concatenate([jnp.where(low, half, 0.0), jnp.where(low, 0.0, half)], 0).astype(BF)

    zero = jnp.zeros((C, C), F32)
    eye = jnp.where(lax.broadcasted_iota(jnp.int32, (C, C), 0) == lanes((C, C)), 1.0, 0.0)

    def both(m):
        return split(jnp.concatenate([jnp.concatenate([m, zero], 1), jnp.concatenate([zero, m], 1)], 0).T)

    r_hi, r_lo = both(rows_ref[...] + eye)
    c_hi, c_lo = both(cols_ref[...] + eye)
    e_hi, e_lo = both(react_ref[...])
    w1_ref[...] = jnp.concatenate([jnp.concatenate([r_hi, c_hi], 1)] * 2, 0)
    w2_ref[...] = jnp.concatenate([r_lo, c_lo], 1)
    w3_ref[...] = jnp.concatenate(
        [jnp.concatenate([e_hi, e_lo], 1), jnp.concatenate([e_hi, jnp.zeros((128, 128), BF)], 1)], 0
    )
    for k in range(OWN):
        put_rates(masks_ref, table_ref, HALO + k, k, 0, brate_ref, burn_ref, bheat_ref)


def put_rates(masks_ref, table_ref, r, k, start, brate_ref, burn_ref, bheat_ref):
    pick = lambda base: (masks_ref[base + r : base + r + 1], masks_ref[base + 63 - r : base + 64 - r])
    hot = onehot(pick(FUEL), pick(BURN), pick(LIT)).T.astype(BF)
    got = jnp.dot(hot, table_ref[...], preferred_element_type=F32)
    at = slice(start, start + COLS)
    brate_ref[k, at], burn_ref[k, at], bheat_ref[k, at] = got[:, 0:128], got[:, 128:256], got[:, 256:384]


def put_edge_rates(edge_ref, table_ref, r0, base_r, starts, brate_ref, burn_ref, bheat_ref):
    rows = []
    for base in (FUEL, BURN, LIT):
        halves = []
        for h in range(2):
            total = None
            for k in range(8):
                p = r0 + k if h == 0 else 63 - r0 - k
                part = edge_ref[base + p : base + p + 1]
                part = pltpu.roll(part, 16 * k, 1) if k else part
                total = part if total is None else total + part
            halves.append(total)
        rows.append(halves)
    got = jnp.dot(onehot(*rows).T.astype(BF), table_ref[...], preferred_element_type=F32)
    for k in range(8):
        for side, start in zip((0, 8), starts):
            part = got[16 * k + side : 16 * k + side + 8]
            r, at = r0 + k - base_r, slice(start, start + HALO)
            brate_ref[r, at], burn_ref[r, at], bheat_ref[r, at] = part[:, 0:128], part[:, 128:256], part[:, 256:384]


def rates(masks, rate, heat, rows, cols, react):
    cells = ((OWN, COLS, LANES), F32)
    return call(
        rates_kernel, "rates",
        [cells, cells, cells, ((128, 384), BF), ((256, 256), BF), ((128, 256), BF), ((256, 256), BF)],
        [((16, 128), F32)],
    )(masks, rate, heat, rows, cols, react)


def turned_edges(left_ref, right_ref, k):
    both = jnp.concatenate([left_ref[k], right_ref[k], jnp.zeros((112, 128), F32)], 0)
    return both.T


def rows_kernel(
    field_ref, masks_ref, near_ref, far_ref, table_ref,
    out_near_ref, out_far_ref, edge_ref, left_ref, right_ref, up_ref, down_ref,
):
    is_even = even("col")
    left_ref[...] = jnp.where(is_even, far_ref[...], near_ref[...])
    right_ref[...] = jnp.where(is_even, near_ref[...], far_ref[...])
    low = lanes((WIDTH, LANES)) < C

    def tile(k):
        return jnp.concatenate([left_ref[k], field_ref[k], right_ref[k]], 0)

    for t in range(4):
        near, far = tile(t), pltpu.roll(tile(4 + t), C, 1)
        at = slice(t * WIDTH, (t + 1) * WIDTH)
        up_ref[at] = jnp.where(low, near, far)
        down_ref[at] = jnp.where(low, far, near)
    edge_ref[0:128] = turned_edges(left_ref, right_ref, OWN)
    edge_ref[128:256] = turned_edges(left_ref, right_ref, OWN + 1)
    for i, base in enumerate((FUEL, BURN, LIT)):
        for ref, first in ((up_ref, HALO), (down_ref, HALO + ROWS - 8)):
            rows = slice(base + first, base + first + 8)
            ref[MSG + 8 * i : MSG + 8 * i + 8] = masks_ref[rows]
            ref[MSG + 24 + 8 * i : MSG + 32 + 8 * i] = edge_ref[rows]
    row_even = even("row")
    out_near_ref[...] = jnp.where(row_even, down_ref[...], up_ref[...])
    out_far_ref[...] = jnp.where(row_even, up_ref[...], down_ref[...])


def row_messages(field, masks, near, far, table):
    message = ((MSG + 48, LANES), F32)
    side = ((OWN + 2, HALO, LANES), F32)
    return call(
        rows_kernel, "rows", [message, message, ((256, LANES), F32), side, side], [message, message]
    )(field, masks, near, far, table)


class Stage:
    def __init__(self, first, last, second, load, old, store, rate, weights, S, W, T, group):
        self.first, self.last, self.second = first, last, second
        self.load, self.old, self.store, self.rate = load, old, store, rate
        self.weights, self.S, self.W, self.T, self.group = weights, S, W, T, group

    def mix(self, r, n, keep=None):
        w1, w2, w3 = self.weights
        brate, burn, bheat = self.rate
        x = jnp.concatenate([self.load(r + k) for k in range(n)], 0)
        hi, lo = split(x)
        t_hi, t_lo = split(jnp.tanh(x))
        sw = jnp.dot(jnp.concatenate([hi, lo], 1), w1[...], preferred_element_type=F32)
        sw = sw + jnp.dot(hi, w2[...], preferred_element_type=F32)
        tt = jnp.dot(jnp.concatenate([t_hi, t_lo], 1), w3[...], preferred_element_type=F32)
        tt = tt[:, 0:LANES] + tt[:, LANES:]
        for k in range(n):
            at = slice(k * WIDTH, (k + 1) * WIDTH)
            q = r + k
            rest = None
            self.S[q] = sw[at, 0:LANES]
            self.W[q, 8 : 8 + WIDTH] = sw[at, LANES:]
            if self.first <= q < self.last or keep:
                rest = 0.5 * x[at] + (burn(q) * tt[at] + bheat(q))
                self.T[q] = rest
            if q == TILES - 1:
                self.S[q + 1] = pltpu.roll(sw[at, 0:LANES], C, 1)
            if keep:
                keep(q, sw[at, 0:LANES], sw[at, LANES:], rest)

    def post(self, q, s_at, w_at, t_at):
        centre = s_at(q) + w_at(q, 8)
        around = (s_at(q - 1) + s_at(q + 1)) + (w_at(q, 7) + w_at(q, 9))
        g = t_at(q) + self.rate[0](q) * (around - centre - centre)
        self.store(q, 0.5 * (self.old(q) + g) if self.second else g)

    def run(self, end, s_at, w_at, t_at, keep=None):
        r, todo = self.first - 1, self.first
        while r < end:
            n = min(self.group, end - r)
            if 0 < end - r - n < 3:
                n = end - r
            self.mix(r, n, keep)
            r += n
            limit = self.last if r == end else min(self.last, r - 1)
            for q in range(todo, limit):
                self.post(q, s_at, w_at, t_at)
            todo = max(todo, limit)


def beside(side, own):
    return lambda r: jnp.concatenate([side[r - HALO, 0:8], own[r - HALO], side[r - HALO, 8:16]], 0)


def clear_margins(W):
    W[:, 0:8] = jnp.zeros((W.shape[0], 8, LANES), F32)
    W[:, 8 + WIDTH :] = jnp.zeros((W.shape[0], 8, LANES), F32)


def inner_kernel(
    field_ref, left_ref, right_ref, edge_ref, brate_in, burn_in, bheat_in, table_ref, w1, w2, w3,
    A, B, brate, burn, bheat, kept_s, kept_w, kept_t, S, W, T,
):
    clear_margins(W)
    clear_margins(kept_w)
    for r0 in range(HALO, TILES, 8):
        put_edge_rates(edge_ref, table_ref, r0, HALO, (0, 8), brate, burn, bheat)
    rate = [beside(brate, brate_in), beside(burn, burn_in), beside(bheat, bheat_in)]

    def start(r):
        k = r - HALO
        return jnp.concatenate([left_ref[k], field_ref[k], right_ref[k]], 0)

    A[HALO] = start(HALO)
    A[HALO + 1] = start(HALO + 1)
    for s in range(1, STAGES + 1):
        src, dst = (A, B) if s % 2 else (B, A)

        def store(q, value, dst=dst):
            dst[q] = value

        def keep(q, s_value, w_value, t_value, s=s):
            near = q - (HALO + s - 1)
            if near < 2:
                kept_s[s - 1, near] = s_value
            if near == 0:
                kept_w[s - 1, 8 : 8 + WIDTH] = w_value
                kept_t[s - 1] = t_value

        stage = Stage(
            HALO + s, TILES, s % 2 == 0,
            start if s == 1 else (lambda r, src=src: src[r]),
            start if s == 2 else (lambda r, dst=dst: dst[r]),
            store, rate, (w1, w2, w3), S, W, T, INNER_GROUP,
        )
        stage.run(TILES, lambda q: S[q], lambda q, o: W[q, o : o + WIDTH], lambda q: T[q], keep)


def inner(field, left, right, edge, rate_arrays):
    cells = ((TILES, WIDTH, LANES), F32)
    edges = ((OWN, 2 * HALO, LANES), F32)
    return call(
        inner_kernel, "inner",
        [cells, cells, edges, edges, edges, ((STAGES, 2, WIDTH, LANES), F32),
         ((STAGES, WIDTH + 16, LANES), F32), ((STAGES, WIDTH, LANES), F32)],
        [((TILES + 1, WIDTH, LANES), F32), ((TILES, WIDTH + 16, LANES), F32), cells],
    )(field, left, right, edge, *rate_arrays)


def outer_kernel(
    A_in, B_in, brate_side, burn_side, bheat_side, kept_s, kept_w, kept_t, brate_in, burn_in, bheat_in,
    near_ref, far_ref, table_ref, w1, w2, w3,
    out_ref, A, B, brate, burn, bheat, masks, edge, S, W, T,
):
    low = lanes((WIDTH, LANES)) < C
    row_even = even("row")

    def arrived(at):
        near, far = near_ref[at], far_ref[at]
        return jnp.where(row_even, far, near), jnp.where(row_even, near, far)

    for t in range(4):
        top, bottom = arrived(slice(t * WIDTH, (t + 1) * WIDTH))
        A[7 - t] = pltpu.roll(jnp.where(low, bottom, top), C, 1)
        A[3 - t] = jnp.where(low, top, bottom)
    clear_margins(W)
    for i, base in enumerate((FUEL, BURN, LIT)):
        for ref, offset in ((masks, MSG + 8 * i), (edge, MSG + 24 + 8 * i)):
            top, bottom = arrived(slice(offset, offset + 8))
            ref[base : base + 8] = top
            ref[base + HALO + ROWS : base + HEIGHT] = bottom
    for r in range(HALO):
        put_rates(masks, table_ref, r, r, HALO, brate, burn, bheat)
    put_edge_rates(edge, table_ref, 0, 0, (0, HALO + COLS), brate, burn, bheat)

    def reader(near, side, own):
        far = beside(side, own)
        return lambda r: near[r] if r < HALO else far(r)

    rate = [
        reader(brate, brate_side, brate_in), reader(burn, burn_side, burn_in), reader(bheat, bheat_side, bheat_in)
    ]
    for s in range(1, STAGES + 1):
        (src, dst), dst_in = ((A, B), B_in) if s % 2 else ((B, A), A_in)
        edge_tile = HALO + s - 1

        def store(q, value, dst=dst):
            dst[q] = value

        def old(q, dst=dst, dst_in=dst_in, s=s):
            return dst[q] if q < HALO + s - 2 else dst_in[q]

        def load(q, src=src):
            return src[q]

        def s_at(q, e=edge_tile, s=s):
            return S[q] if q < e else kept_s[s - 1, q - e]

        def w_at(q, o, e=edge_tile, s=s):
            return W[q, o : o + WIDTH] if q < e else kept_w[s - 1, o : o + WIDTH]

        def t_at(q, e=edge_tile, s=s):
            return T[q] if q < e else kept_t[s - 1]

        stage = Stage(
            s, HALO + s, s % 2 == 0, load, old, store, rate, (w1, w2, w3), S, W, T, OUTER_GROUP
        )
        stage.run(edge_tile, s_at, w_at, t_at)
    flat = out_ref.reshape(C * ROWS, COLS)
    for k in reversed(range(OWN)):
        r = HALO + k
        turned = (A if r < 2 * HALO else A_in)[r, HALO : HALO + COLS].T
        flat[pl.ds(k, C, stride=ROWS), :] = turned[0:C]
        flat[pl.ds(ROWS - 1 - k, C, stride=ROWS), :] = turned[C:]


def outer(states, rate_arrays, near, far):
    few = 2 * HALO
    cells = ((few, WIDTH, LANES), F32)
    edge_cells = ((HALO, WIDTH, LANES), F32)
    return call(
        outer_kernel, "outer", [((C, ROWS, COLS), F32)],
        [cells, cells, edge_cells, edge_cells, edge_cells, ((192, COLS), F32), ((192, COLS), F32),
         cells, ((few, WIDTH + 16, LANES), F32), cells],
    )(*states, *rate_arrays[:3], near, far, *rate_arrays[3:])[0]


def exchange(near, far, axis):
    size = lax.axis_size(axis)

    def swap(x, start):
        pairs = [(i, i + 1) for i in range(start, size - 1, 2)]
        return lax.ppermute(x, axis, pairs + [(b, a) for a, b in pairs])

    far = swap(far, 1)
    return swap(near, 0), far


def per_device(
    fire_state, fuel_class, firebreak, ignition,
    spread_rate, spread_rows, spread_cols, reaction, ignition_heat,
):
    field, masks, near, far = pack(fire_state, fuel_class, firebreak, ignition)
    near, far = exchange(near, far, "col")
    rate_arrays = rates(masks, spread_rate, ignition_heat[None], spread_rows, spread_cols, reaction)
    near, far, edge, left, right = row_messages(field, masks, near, far, rate_arrays[3])
    near, far = exchange(near, far, "row")
    states = inner(field, left, right, edge, rate_arrays)
    return outer(states, rate_arrays, near, far)


def solution(mesh):
    whole = P(None, "row", "col")
    cells = P("row", "col")
    return jax.shard_map(
        per_device,
        mesh=mesh,
        in_specs=(whole, cells, cells, cells, P(), P(), P(), P(), P()),
        out_specs=whole,
        check_vma=False,
    )
```

```python
import jax
import jax.numpy as jnp
from jax import lax
from jax.experimental import pallas as pl
from jax.experimental.pallas import tpu as pltpu
from jax.sharding import PartitionSpec as P

ITERS = 4
STAGES = 2 * ITERS
HALO = STAGES
C, ROWS, COLS = 64, 48, 128
HEIGHT = ROWS + 2 * HALO
WIDTH = COLS + 2 * HALO
TILES = HEIGHT // 2
OWN = TILES - HALO
LANES = 2 * C
INNER_GROUP = 8
OUTER_GROUP = 4
MSG = 4 * WIDTH
BF = jnp.bfloat16
F32 = jnp.float32


def split(x):
    hi = x.astype(BF)
    return hi, (x - hi.astype(F32)).astype(BF)


def lanes(shape):
    return lax.broadcasted_iota(jnp.int32, shape, len(shape) - 1)


def call(kernel, name, outs, scratch=(), limit=12, from_hbm=0, extra=()):
    specs = {"in_specs": [pl.BlockSpec(memory_space=pltpu.HBM)] * from_hbm} if from_hbm else {}
    return pl.pallas_call(
        kernel,
        name=name,
        out_shape=[jax.ShapeDtypeStruct(s, d) for s, d in outs],
        scratch_shapes=[pltpu.VMEM(s, d) for s, d in scratch] + list(extra),
        **specs,
        compiler_params=pltpu.CompilerParams(vmem_limit_bytes=limit * 2**20),
    )


FUEL, BURN, LIT = 0, HEIGHT, 2 * HEIGHT


def even(axis):
    return lax.rem(lax.axis_index(axis), 2) == 0


def pack_kernel(
    x_hbm, fuel_hbm, break_hbm, lit_hbm, field_ref, masks_ref, near_ref, far_ref, x_ref, ints, sems
):
    copies = [
        pltpu.make_async_copy(x_hbm.at[:, pl.ds(8 * g, 8), :], x_ref.at[:, pl.ds(8 * g, 8), :], sems.at[g])
        for g in range(ROWS // 8)
    ]
    for g in (0, 5, 1, 4, 2, 3):
        copies[g].start()
    small = [
        pltpu.make_async_copy(ref, ints.at[i], sems.at[6 + i])
        for i, ref in enumerate((fuel_hbm, break_hbm, lit_hbm))
    ]
    for copy in small:
        copy.start()
    masks_ref[...] = jnp.zeros_like(masks_ref)
    flat = x_ref.reshape(C * ROWS, COLS)
    is_even = even("col")

    def messages(k, turned):
        first, last = turned[0:HALO], turned[COLS - HALO :]
        near_ref[k] = jnp.where(is_even, last, first)
        far_ref[k] = jnp.where(is_even, first, last)

    for k in range(OWN):
        if k % 8 == 0:
            copies[k // 8].wait()
            copies[5 - k // 8].wait()
        top = flat[pl.ds(k, C, stride=ROWS), :]
        bottom = flat[pl.ds(ROWS - 1 - k, C, stride=ROWS), :]
        turned = jnp.concatenate([top, bottom], 0).T
        field_ref[k] = turned
        messages(k, turned)
    for copy in small:
        copy.wait()
    masks_ref[FUEL + HALO : FUEL + HALO + ROWS] = ints[0].astype(F32)
    masks_ref[BURN + HALO : BURN + HALO + ROWS] = (1 - ints[1]).astype(F32)
    masks_ref[LIT + HALO : LIT + HALO + ROWS] = ints[2].astype(F32)
    messages(OWN, masks_ref[0:128].T)
    messages(OWN + 1, masks_ref[128:256].T)


def pack(x, fuel, firebreak, lit):
    message = ((OWN + 2, HALO, LANES), F32)
    return call(
        pack_kernel, "pack", [((OWN, COLS, LANES), F32), ((256, COLS), F32), message, message],
        [((C, ROWS, COLS), F32)], from_hbm=4,
        extra=[pltpu.VMEM((3, ROWS, COLS), jnp.int32), pltpu.SemaphoreType.DMA((9,))],
    )(*[pltpu.with_memory_space_constraint(a, pltpu.HBM) for a in (x, fuel, firebreak, lit)])


def onehot(fuel, burn, lit):
    slot = lax.broadcasted_iota(jnp.int32, (C, 128), 0)
    cls = (slot & 15).astype(F32)
    halves = []
    for f, b, i in zip(fuel, burn, lit):
        picked = jnp.where((cls == f) | (cls == 13.0), b, jnp.where(cls == 14.0, b * i, 0.0))
        halves.append(jnp.where(slot < 32, picked, 0.0))
    return jnp.concatenate(halves, 0)


def rates_kernel(
    masks_ref, rate_ref, heat_ref, rows_ref, cols_ref, react_ref, field_ref,
    brate_ref, burn_ref, bheat_ref, table_ref, w1_ref, w2_ref, w3_ref, s_ref, w_ref, t_ref, tab,
):
    tab[...] = jnp.zeros_like(tab)
    tab[0:13, 0:64] = rate_ref[...]
    tab[14:15, 0:64] = heat_ref[...]
    t = tab[...]
    t = t + pltpu.roll(t, 64, 1)
    row = lax.broadcasted_iota(jnp.int32, (16, 128), 0)
    h = jnp.concatenate(
        [jnp.where(row < 13, t, 0.0), jnp.where(row == 13, 1.0, 0.0), jnp.where(row == 14, t, 0.0)], 1
    )
    hi, lo = split(h)
    half = jnp.concatenate([hi.astype(F32), lo.astype(F32), jnp.zeros((32, 384), F32)], 0)
    low = (lanes((64, 384)) & 127) < 64
    table_ref[...] = jnp.concatenate([jnp.where(low, half, 0.0), jnp.where(low, 0.0, half)], 0).astype(BF)

    zero = jnp.zeros((C, C), F32)
    eye = jnp.where(lax.broadcasted_iota(jnp.int32, (C, C), 0) == lanes((C, C)), 1.0, 0.0)

    def both(m):
        return split(jnp.concatenate([jnp.concatenate([m, zero], 1), jnp.concatenate([zero, m], 1)], 0).T)

    r_hi, r_lo = both(rows_ref[...] + eye)
    c_hi, c_lo = both(cols_ref[...] + eye)
    e_hi, e_lo = both(react_ref[...])
    w1_ref[...] = jnp.concatenate([jnp.concatenate([r_hi, c_hi], 1)] * 2, 0)
    w2_ref[...] = jnp.concatenate([r_lo, c_lo], 1)
    w3_ref[...] = jnp.concatenate(
        [jnp.concatenate([e_hi, e_lo], 1), jnp.concatenate([e_hi, jnp.zeros((128, 128), BF)], 1)], 0
    )
    for k in range(OWN):
        put_rates(masks_ref, table_ref, HALO + k, k, 0, brate_ref, burn_ref, bheat_ref)
    for k0 in range(0, OWN, INNER_GROUP):
        x = field_ref[k0 : k0 + INNER_GROUP].reshape(INNER_GROUP * COLS, LANES)
        s_all, w_all, tt = mixed(x, (w1_ref, w2_ref, w3_ref))
        for i in range(INNER_GROUP):
            k, at = k0 + i, slice(i * COLS, (i + 1) * COLS)
            s_ref[k], w_ref[k] = s_all[at], w_all[at]
            t_ref[k] = 0.5 * x[at] + (burn_ref[k] * tt[at] + bheat_ref[k])


def mixed(x, weights):
    w1, w2, w3 = weights
    hi, lo = split(x)
    t_hi, t_lo = split(jnp.tanh(x))
    sw = jnp.dot(jnp.concatenate([hi, lo], 1), w1[...], preferred_element_type=F32)
    sw = sw + jnp.dot(hi, w2[...], preferred_element_type=F32)
    tt = jnp.dot(jnp.concatenate([t_hi, t_lo], 1), w3[...], preferred_element_type=F32)
    return sw[:, 0:LANES], sw[:, LANES:], tt[:, 0:LANES] + tt[:, LANES:]


def put_rates(masks_ref, table_ref, r, k, start, brate_ref, burn_ref, bheat_ref):
    pick = lambda base: (masks_ref[base + r : base + r + 1], masks_ref[base + 63 - r : base + 64 - r])
    hot = onehot(pick(FUEL), pick(BURN), pick(LIT)).T.astype(BF)
    got = jnp.dot(hot, table_ref[...], preferred_element_type=F32)
    at = slice(start, start + COLS)
    brate_ref[k, at], burn_ref[k, at], bheat_ref[k, at] = got[:, 0:128], got[:, 128:256], got[:, 256:384]


def put_edge_rates(edge_ref, table_ref, r0, base_r, starts, brate_ref, burn_ref, bheat_ref):
    rows = []
    for base in (FUEL, BURN, LIT):
        halves = []
        for h in range(2):
            total = None
            for k in range(8):
                p = r0 + k if h == 0 else 63 - r0 - k
                part = edge_ref[base + p : base + p + 1]
                part = pltpu.roll(part, 16 * k, 1) if k else part
                total = part if total is None else total + part
            halves.append(total)
        rows.append(halves)
    got = jnp.dot(onehot(*rows).T.astype(BF), table_ref[...], preferred_element_type=F32)
    for k in range(8):
        for side, start in zip((0, 8), starts):
            part = got[16 * k + side : 16 * k + side + 8]
            r, at = r0 + k - base_r, slice(start, start + HALO)
            brate_ref[r, at], burn_ref[r, at], bheat_ref[r, at] = part[:, 0:128], part[:, 128:256], part[:, 256:384]


def rates(masks, rate, heat, rows, cols, react, field):
    cells = ((OWN, COLS, LANES), F32)
    return call(
        rates_kernel, "rates",
        [cells, cells, cells, ((128, 384), BF), ((256, 256), BF), ((128, 256), BF), ((256, 256), BF),
         cells, cells, cells],
        [((16, 128), F32)],
    )(masks, rate, heat, rows, cols, react, field)


def turned_edges(left_ref, right_ref, k):
    both = jnp.concatenate([left_ref[k], right_ref[k], jnp.zeros((112, 128), F32)], 0)
    return both.T


def rows_kernel(
    field_ref, masks_ref, near_ref, far_ref, table_ref,
    out_near_ref, out_far_ref, edge_ref, left_ref, right_ref, up_ref, down_ref,
):
    is_even = even("col")
    left_ref[...] = jnp.where(is_even, far_ref[...], near_ref[...])
    right_ref[...] = jnp.where(is_even, near_ref[...], far_ref[...])
    low = lanes((WIDTH, LANES)) < C

    def tile(k):
        return jnp.concatenate([left_ref[k], field_ref[k], right_ref[k]], 0)

    for t in range(4):
        near, far = tile(t), pltpu.roll(tile(4 + t), C, 1)
        at = slice(t * WIDTH, (t + 1) * WIDTH)
        up_ref[at] = jnp.where(low, near, far)
        down_ref[at] = jnp.where(low, far, near)
    edge_ref[0:128] = turned_edges(left_ref, right_ref, OWN)
    edge_ref[128:256] = turned_edges(left_ref, right_ref, OWN + 1)
    for i, base in enumerate((FUEL, BURN, LIT)):
        for ref, first in ((up_ref, HALO), (down_ref, HALO + ROWS - 8)):
            rows = slice(base + first, base + first + 8)
            ref[MSG + 8 * i : MSG + 8 * i + 8] = masks_ref[rows]
            ref[MSG + 24 + 8 * i : MSG + 32 + 8 * i] = edge_ref[rows]
    row_even = even("row")
    out_near_ref[...] = jnp.where(row_even, down_ref[...], up_ref[...])
    out_far_ref[...] = jnp.where(row_even, up_ref[...], down_ref[...])


def row_messages(field, masks, near, far, table):
    message = ((MSG + 48, LANES), F32)
    side = ((OWN + 2, HALO, LANES), F32)
    return call(
        rows_kernel, "rows", [message, message, ((256, LANES), F32), side, side], [message, message]
    )(field, masks, near, far, table)


class Stage:
    def __init__(self, first, last, second, load, old, store, rate, weights, S, W, T, group):
        self.first, self.last, self.second = first, last, second
        self.load, self.old, self.store, self.rate = load, old, store, rate
        self.weights, self.S, self.W, self.T, self.group = weights, S, W, T, group

    def mix(self, r, n, keep=None):
        brate, burn, bheat = self.rate
        x = jnp.concatenate([self.load(r + k) for k in range(n)], 0)
        s_all, w_all, tt = mixed(x, self.weights)
        for k in range(n):
            at = slice(k * WIDTH, (k + 1) * WIDTH)
            q = r + k
            rest = None
            self.S[q] = s_all[at]
            self.W[q, 8 : 8 + WIDTH] = w_all[at]
            if self.first <= q < self.last or keep:
                rest = 0.5 * x[at] + (burn(q) * tt[at] + bheat(q))
                self.T[q] = rest
            if q == TILES - 1:
                self.S[q + 1] = pltpu.roll(s_all[at], C, 1)
            if keep:
                keep(q, s_all[at], w_all[at], rest)

    def post(self, q, s_at, w_at, t_at):
        centre = s_at(q) + w_at(q, 8)
        around = (s_at(q - 1) + s_at(q + 1)) + (w_at(q, 7) + w_at(q, 9))
        g = t_at(q) + self.rate[0](q) * (around - centre - centre)
        self.store(q, 0.5 * (self.old(q) + g) if self.second else g)

    def run(self, end, s_at, w_at, t_at, keep=None, before=None):
        r, todo = self.first - 1, self.first
        while r < end:
            n = min(self.group, end - r)
            if 0 < end - r - n < 3:
                n = end - r
            if before:
                before(r + n)
            self.mix(r, n, keep)
            r += n
            limit = self.last if r == end else min(self.last, r - 1)
            for q in range(todo, limit):
                self.post(q, s_at, w_at, t_at)
            todo = max(todo, limit)


def beside(side, own):
    return lambda r: jnp.concatenate([side[r - HALO, 0:8], own[r - HALO], side[r - HALO, 8:16]], 0)


def clear_margins(W):
    W[:, 0:8] = jnp.zeros((W.shape[0], 8, LANES), F32)
    W[:, 8 + WIDTH :] = jnp.zeros((W.shape[0], 8, LANES), F32)


def inner_kernel(
    field_ref, left_ref, right_ref, edge_ref, brate_in, burn_in, bheat_in, table_ref, w1, w2, w3,
    s_in, w_in, t_in, A, B, brate, burn, bheat, kept_s, kept_w, kept_t, S, W, T, side_s, side_t, W1,
):
    clear_margins(W)
    clear_margins(W1)
    clear_margins(kept_w)
    for r0 in range(HALO, TILES, 8):
        put_edge_rates(edge_ref, table_ref, r0, HALO, (0, 8), brate, burn, bheat)
    rate = [beside(brate, brate_in), beside(burn, burn_in), beside(bheat, bheat_in)]

    def start(r):
        k = r - HALO
        return jnp.concatenate([left_ref[k], field_ref[k], right_ref[k]], 0)

    x = jnp.concatenate([ref[k] for k in range(OWN) for ref in (left_ref, right_ref)], 0)
    s_all, w_all, tt = mixed(x, (w1, w2, w3))
    for k in range(OWN):
        r, span = HALO + k, slice(16 * k, 16 * k + 16)
        side_s[k] = s_all[span]
        side_t[k] = 0.5 * x[span] + (burn[k] * tt[span] + bheat[k])
        W1[r, 8:16] = w_all[span][0:8]
        W1[r, 16 + COLS : 24 + COLS] = w_all[span][8:16]

    def first_w(k):
        W1[HALO + k, 16 : 16 + COLS] = w_in[k]

    s_of, t_first = beside(side_s, s_in), beside(side_t, t_in)

    def s_first(q):
        return s_of(q) if q < TILES else pltpu.roll(s_of(TILES - 1), C, 1)

    def w_first(q, o):
        return W1[q, o : o + WIDTH]

    A[HALO] = start(HALO)
    A[HALO + 1] = start(HALO + 1)
    for s in range(1, STAGES + 1):
        src, dst = (A, B) if s % 2 else (B, A)

        def store(q, value, dst=dst):
            dst[q] = value

        def keep(q, s_value, w_value, t_value, s=s):
            near = q - (HALO + s - 1)
            if near < 2:
                kept_s[s - 1, near] = s_value
            if near == 0:
                kept_w[s - 1, 8 : 8 + WIDTH] = w_value
                kept_t[s - 1] = t_value

        stage = Stage(
            HALO + s, TILES, s % 2 == 0,
            lambda r, src=src: src[r],
            start if s == 2 else (lambda r, dst=dst: dst[r]),
            store, rate, (w1, w2, w3), S, W, T, INNER_GROUP,
        )
        readers = (lambda q: S[q], lambda q, o: W[q, o : o + WIDTH], lambda q: T[q])
        if s == 1:
            first_w(0)
            first_w(1)
            for q in (HALO, HALO + 1):
                keep(q, s_first(q), W1[q, 8 : 8 + WIDTH], t_first(q))
            opening, finished = stage, [HALO + 1]
            continue

        def before(end):
            for q in range(finished[0], end):
                first_w(q - HALO)
                opening.post(q, s_first, w_first, t_first)
            finished[0] = max(finished[0], end)

        stage.run(TILES, *readers, keep, before if s == 2 else None)


def inner(field, left, right, edge, rate_arrays):
    cells = ((TILES, WIDTH, LANES), F32)
    edges = ((OWN, 2 * HALO, LANES), F32)
    return call(
        inner_kernel, "inner",
        [cells, cells, edges, edges, edges, ((STAGES, 2, WIDTH, LANES), F32),
         ((STAGES, WIDTH + 16, LANES), F32), ((STAGES, WIDTH, LANES), F32)],
        [((TILES + 1, WIDTH, LANES), F32), ((TILES, WIDTH + 16, LANES), F32), cells, edges, edges,
         ((TILES, WIDTH + 16, LANES), F32)], limit=20,
    )(field, left, right, edge, *rate_arrays)


def outer_kernel(
    A_in, B_in, brate_side, burn_side, bheat_side, kept_s, kept_w, kept_t, brate_in, burn_in, bheat_in,
    near_ref, far_ref, table_ref, w1, w2, w3,
    out_ref, A, B, brate, burn, bheat, masks, edge, S, W, T,
):
    low = lanes((WIDTH, LANES)) < C
    row_even = even("row")

    def arrived(at):
        near, far = near_ref[at], far_ref[at]
        return jnp.where(row_even, far, near), jnp.where(row_even, near, far)

    for t in range(4):
        top, bottom = arrived(slice(t * WIDTH, (t + 1) * WIDTH))
        A[7 - t] = pltpu.roll(jnp.where(low, bottom, top), C, 1)
        A[3 - t] = jnp.where(low, top, bottom)
    clear_margins(W)
    for i, base in enumerate((FUEL, BURN, LIT)):
        for ref, offset in ((masks, MSG + 8 * i), (edge, MSG + 24 + 8 * i)):
            top, bottom = arrived(slice(offset, offset + 8))
            ref[base : base + 8] = top
            ref[base + HALO + ROWS : base + HEIGHT] = bottom
    for r in range(HALO):
        put_rates(masks, table_ref, r, r, HALO, brate, burn, bheat)
    put_edge_rates(edge, table_ref, 0, 0, (0, HALO + COLS), brate, burn, bheat)

    def reader(near, side, own):
        far = beside(side, own)
        return lambda r: near[r] if r < HALO else far(r)

    rate = [
        reader(brate, brate_side, brate_in), reader(burn, burn_side, burn_in), reader(bheat, bheat_side, bheat_in)
    ]
    for s in range(1, STAGES + 1):
        (src, dst), dst_in = ((A, B), B_in) if s % 2 else ((B, A), A_in)
        edge_tile = HALO + s - 1

        def store(q, value, dst=dst):
            dst[q] = value

        def old(q, dst=dst, dst_in=dst_in, s=s):
            return dst[q] if q < HALO + s - 2 else dst_in[q]

        def load(q, src=src):
            return src[q]

        def s_at(q, e=edge_tile, s=s):
            return S[q] if q < e else kept_s[s - 1, q - e]

        def w_at(q, o, e=edge_tile, s=s):
            return W[q, o : o + WIDTH] if q < e else kept_w[s - 1, o : o + WIDTH]

        def t_at(q, e=edge_tile, s=s):
            return T[q] if q < e else kept_t[s - 1]

        stage = Stage(
            s, HALO + s, s % 2 == 0, load, old, store, rate, (w1, w2, w3), S, W, T, OUTER_GROUP
        )
        stage.run(edge_tile, s_at, w_at, t_at)
    flat = out_ref.reshape(C * ROWS, COLS)
    for k in reversed(range(OWN)):
        r = HALO + k
        turned = (A if r < 2 * HALO else A_in)[r, HALO : HALO + COLS].T
        flat[pl.ds(k, C, stride=ROWS), :] = turned[0:C]
        flat[pl.ds(ROWS - 1 - k, C, stride=ROWS), :] = turned[C:]


def outer(states, rate_arrays, near, far):
    few = 2 * HALO
    cells = ((few, WIDTH, LANES), F32)
    edge_cells = ((HALO, WIDTH, LANES), F32)
    return call(
        outer_kernel, "outer", [((C, ROWS, COLS), F32)],
        [cells, cells, edge_cells, edge_cells, edge_cells, ((192, COLS), F32), ((192, COLS), F32),
         cells, ((few, WIDTH + 16, LANES), F32), cells],
    )(*states, *rate_arrays[:3], near, far, *rate_arrays[3:7])[0]


def exchange(near, far, axis):
    size = lax.axis_size(axis)

    def swap(x, start):
        pairs = [(i, i + 1) for i in range(start, size - 1, 2)]
        return lax.ppermute(x, axis, pairs + [(b, a) for a, b in pairs])

    far = swap(far, 1)
    return swap(near, 0), far


def per_device(
    fire_state, fuel_class, firebreak, ignition,
    spread_rate, spread_rows, spread_cols, reaction, ignition_heat,
):
    field, masks, near, far = pack(fire_state, fuel_class, firebreak, ignition)
    near, far = exchange(near, far, "col")
    rate_arrays = rates(
        masks, spread_rate, ignition_heat[None], spread_rows, spread_cols, reaction, field
    )
    near, far, edge, left, right = row_messages(field, masks, near, far, rate_arrays[3])
    near, far = exchange(near, far, "row")
    states = inner(field, left, right, edge, rate_arrays)
    return outer(states, rate_arrays, near, far)


def solution(mesh):
    whole = P(None, "row", "col")
    cells = P("row", "col")
    return jax.shard_map(
        per_device,
        mesh=mesh,
        in_specs=(whole, cells, cells, cells, P(), P(), P(), P(), P()),
        out_specs=whole,
        check_vma=False,
    )
```

```python
import jax
import jax.numpy as jnp
from jax import lax
from jax.experimental import pallas as pl
from jax.experimental.pallas import tpu as pltpu
from jax.sharding import PartitionSpec as P

ITERS = 4
STAGES = 2 * ITERS
HALO = STAGES
C, ROWS, COLS = 64, 48, 128
HEIGHT = ROWS + 2 * HALO
WIDTH = COLS + 2 * HALO
TILES = HEIGHT // 2
OWN = TILES - HALO
LANES = 2 * C
INNER_GROUP = 8
OUTER_GROUP = 4
MSG = 4 * WIDTH
MIDDLE = COLS - 16
BF = jnp.bfloat16
F32 = jnp.float32


def split(x):
    hi = x.astype(BF)
    return hi, (x - hi.astype(F32)).astype(BF)


def lanes(shape):
    return lax.broadcasted_iota(jnp.int32, shape, len(shape) - 1)


def call(kernel, name, outs, scratch=(), limit=12, from_hbm=0, extra=()):
    specs = {"in_specs": [pl.BlockSpec(memory_space=pltpu.HBM)] * from_hbm} if from_hbm else {}
    return pl.pallas_call(
        kernel,
        name=name,
        out_shape=[jax.ShapeDtypeStruct(s, d) for s, d in outs],
        scratch_shapes=[pltpu.VMEM(s, d) for s, d in scratch] + list(extra),
        **specs,
        compiler_params=pltpu.CompilerParams(vmem_limit_bytes=limit * 2**20),
    )


FUEL, BURN, LIT = 0, HEIGHT, 2 * HEIGHT


def even(axis):
    return lax.rem(lax.axis_index(axis), 2) == 0


def pack_kernel(
    x_hbm, fuel_hbm, break_hbm, lit_hbm, field_ref, masks_ref, near_ref, far_ref, x_ref, ints, sems
):
    copies = [
        pltpu.make_async_copy(x_hbm.at[:, pl.ds(8 * g, 8), :], x_ref.at[:, pl.ds(8 * g, 8), :], sems.at[g])
        for g in range(ROWS // 8)
    ]
    for g in (0, 5, 1, 4, 2, 3):
        copies[g].start()
    small = [
        pltpu.make_async_copy(ref, ints.at[i], sems.at[6 + i])
        for i, ref in enumerate((fuel_hbm, break_hbm, lit_hbm))
    ]
    for copy in small:
        copy.start()
    masks_ref[...] = jnp.zeros_like(masks_ref)
    flat = x_ref.reshape(C * ROWS, COLS)
    is_even = even("col")

    def messages(k, turned):
        first, last = turned[0:HALO], turned[COLS - HALO :]
        near_ref[k] = jnp.where(is_even, last, first)
        far_ref[k] = jnp.where(is_even, first, last)

    for k in range(OWN):
        if k % 8 == 0:
            copies[k // 8].wait()
            copies[5 - k // 8].wait()
        top = flat[pl.ds(k, C, stride=ROWS), :]
        bottom = flat[pl.ds(ROWS - 1 - k, C, stride=ROWS), :]
        turned = jnp.concatenate([top, bottom], 0).T
        field_ref[k] = turned
        messages(k, turned)
    for copy in small:
        copy.wait()
    masks_ref[FUEL + HALO : FUEL + HALO + ROWS] = ints[0].astype(F32)
    masks_ref[BURN + HALO : BURN + HALO + ROWS] = (1 - ints[1]).astype(F32)
    masks_ref[LIT + HALO : LIT + HALO + ROWS] = ints[2].astype(F32)
    messages(OWN, masks_ref[0:128].T)
    messages(OWN + 1, masks_ref[128:256].T)


def pack(x, fuel, firebreak, lit):
    message = ((OWN + 2, HALO, LANES), F32)
    return call(
        pack_kernel, "pack", [((OWN, COLS, LANES), F32), ((256, COLS), F32), message, message],
        [((C, ROWS, COLS), F32)], from_hbm=4,
        extra=[pltpu.VMEM((3, ROWS, COLS), jnp.int32), pltpu.SemaphoreType.DMA((9,))],
    )(*[pltpu.with_memory_space_constraint(a, pltpu.HBM) for a in (x, fuel, firebreak, lit)])


def onehot(fuel, burn, lit):
    slot = lax.broadcasted_iota(jnp.int32, (C, 128), 0)
    cls = (slot & 15).astype(F32)
    halves = []
    for f, b, i in zip(fuel, burn, lit):
        picked = jnp.where((cls == f) | (cls == 13.0), b, jnp.where(cls == 14.0, b * i, 0.0))
        halves.append(jnp.where(slot < 32, picked, 0.0))
    return jnp.concatenate(halves, 0)


def rates_kernel(
    masks_ref, rate_ref, heat_ref, rows_ref, cols_ref, react_ref, field_ref,
    brate_ref, burn_ref, bheat_ref, table_ref, w1_ref, w2_ref, w3_ref, s_ref, w_ref, t_ref,
    s2_ref, w2nd_ref, t2_ref, tab,
):
    tab[...] = jnp.zeros_like(tab)
    tab[0:13, 0:64] = rate_ref[...]
    tab[14:15, 0:64] = heat_ref[...]
    t = tab[...]
    t = t + pltpu.roll(t, 64, 1)
    row = lax.broadcasted_iota(jnp.int32, (16, 128), 0)
    h = jnp.concatenate(
        [jnp.where(row < 13, t, 0.0), jnp.where(row == 13, 1.0, 0.0), jnp.where(row == 14, t, 0.0)], 1
    )
    hi, lo = split(h)
    half = jnp.concatenate([hi.astype(F32), lo.astype(F32), jnp.zeros((32, 384), F32)], 0)
    low = (lanes((64, 384)) & 127) < 64
    table_ref[...] = jnp.concatenate([jnp.where(low, half, 0.0), jnp.where(low, 0.0, half)], 0).astype(BF)

    zero = jnp.zeros((C, C), F32)
    eye = jnp.where(lax.broadcasted_iota(jnp.int32, (C, C), 0) == lanes((C, C)), 1.0, 0.0)

    def both(m):
        return split(jnp.concatenate([jnp.concatenate([m, zero], 1), jnp.concatenate([zero, m], 1)], 0).T)

    r_hi, r_lo = both(rows_ref[...] + eye)
    c_hi, c_lo = both(cols_ref[...] + eye)
    e_hi, e_lo = both(react_ref[...])
    w1_ref[...] = jnp.concatenate([jnp.concatenate([r_hi, c_hi], 1)] * 2, 0)
    w2_ref[...] = jnp.concatenate([r_lo, c_lo], 1)
    w3_ref[...] = jnp.concatenate(
        [jnp.concatenate([e_hi, e_lo], 1), jnp.concatenate([e_hi, jnp.zeros((128, 128), BF)], 1)], 0
    )
    for k in range(OWN):
        put_rates(masks_ref, table_ref, HALO + k, k, 0, brate_ref, burn_ref, bheat_ref)
    for k0 in range(0, OWN, INNER_GROUP):
        x = field_ref[k0 : k0 + INNER_GROUP].reshape(INNER_GROUP * COLS, LANES)
        s_all, w_all, tt = mixed(x, (w1_ref, w2_ref, w3_ref))
        for i in range(INNER_GROUP):
            k, at = k0 + i, slice(i * COLS, (i + 1) * COLS)
            s_ref[k], w_ref[k] = s_all[at], w_all[at]
            t_ref[k] = 0.5 * x[at] + (burn_ref[k] * tt[at] + bheat_ref[k])
    mid = slice(8, 8 + MIDDLE)

    def s_mid(k):
        return s_ref[k, mid] if k < OWN else pltpu.roll(s_ref[OWN - 1, mid], C, 1)

    for k0, n in ((1, 7), (8, 8), (16, 8)):
        xs = []
        for k in range(k0, k0 + n):
            centre = s_mid(k) + w_ref[k, mid]
            around = (s_mid(k - 1) + s_mid(k + 1)) + (w_ref[k, 7 : 7 + MIDDLE] + w_ref[k, 9 : 9 + MIDDLE])
            xs.append(t_ref[k, mid] + brate_ref[k, mid] * (around - centre - centre))
        s_all, w_all, tt = mixed(jnp.concatenate(xs, 0), (w1_ref, w2_ref, w3_ref))
        for i, x in enumerate(xs):
            k, at = k0 + i, slice(i * MIDDLE, (i + 1) * MIDDLE)
            s2_ref[k], w2nd_ref[k] = s_all[at], w_all[at]
            t2_ref[k] = 0.5 * x + (burn_ref[k, mid] * tt[at] + bheat_ref[k, mid])


def mixed(x, weights):
    w1, w2, w3 = weights
    hi, lo = split(x)
    t_hi, t_lo = split(jnp.tanh(x))
    sw = jnp.dot(jnp.concatenate([hi, lo], 1), w1[...], preferred_element_type=F32)
    sw = sw + jnp.dot(hi, w2[...], preferred_element_type=F32)
    tt = jnp.dot(jnp.concatenate([t_hi, t_lo], 1), w3[...], preferred_element_type=F32)
    return sw[:, 0:LANES], sw[:, LANES:], tt[:, 0:LANES] + tt[:, LANES:]


def put_rates(masks_ref, table_ref, r, k, start, brate_ref, burn_ref, bheat_ref):
    pick = lambda base: (masks_ref[base + r : base + r + 1], masks_ref[base + 63 - r : base + 64 - r])
    hot = onehot(pick(FUEL), pick(BURN), pick(LIT)).T.astype(BF)
    got = jnp.dot(hot, table_ref[...], preferred_element_type=F32)
    at = slice(start, start + COLS)
    brate_ref[k, at], burn_ref[k, at], bheat_ref[k, at] = got[:, 0:128], got[:, 128:256], got[:, 256:384]


def put_edge_rates(edge_ref, table_ref, r0, base_r, starts, brate_ref, burn_ref, bheat_ref):
    rows = []
    for base in (FUEL, BURN, LIT):
        halves = []
        for h in range(2):
            total = None
            for k in range(8):
                p = r0 + k if h == 0 else 63 - r0 - k
                part = edge_ref[base + p : base + p + 1]
                part = pltpu.roll(part, 16 * k, 1) if k else part
                total = part if total is None else total + part
            halves.append(total)
        rows.append(halves)
    got = jnp.dot(onehot(*rows).T.astype(BF), table_ref[...], preferred_element_type=F32)
    for k in range(8):
        for side, start in zip((0, 8), starts):
            part = got[16 * k + side : 16 * k + side + 8]
            r, at = r0 + k - base_r, slice(start, start + HALO)
            brate_ref[r, at], burn_ref[r, at], bheat_ref[r, at] = part[:, 0:128], part[:, 128:256], part[:, 256:384]


def rates(masks, rate, heat, rows, cols, react, field):
    cells = ((OWN, COLS, LANES), F32)
    middle = ((OWN, MIDDLE, LANES), F32)
    return call(
        rates_kernel, "rates",
        [cells, cells, cells, ((128, 384), BF), ((256, 256), BF), ((128, 256), BF), ((256, 256), BF),
         cells, cells, cells, middle, middle, middle],
        [((16, 128), F32)],
    )(masks, rate, heat, rows, cols, react, field)


def turned_edges(left_ref, right_ref, k):
    both = jnp.concatenate([left_ref[k], right_ref[k], jnp.zeros((112, 128), F32)], 0)
    return both.T


def rows_kernel(
    field_ref, masks_ref, near_ref, far_ref, table_ref,
    out_near_ref, out_far_ref, edge_ref, left_ref, right_ref, up_ref, down_ref,
):
    is_even = even("col")
    left_ref[...] = jnp.where(is_even, far_ref[...], near_ref[...])
    right_ref[...] = jnp.where(is_even, near_ref[...], far_ref[...])
    low = lanes((WIDTH, LANES)) < C

    def tile(k):
        return jnp.concatenate([left_ref[k], field_ref[k], right_ref[k]], 0)

    for t in range(4):
        near, far = tile(t), pltpu.roll(tile(4 + t), C, 1)
        at = slice(t * WIDTH, (t + 1) * WIDTH)
        up_ref[at] = jnp.where(low, near, far)
        down_ref[at] = jnp.where(low, far, near)
    edge_ref[0:128] = turned_edges(left_ref, right_ref, OWN)
    edge_ref[128:256] = turned_edges(left_ref, right_ref, OWN + 1)
    for i, base in enumerate((FUEL, BURN, LIT)):
        for ref, first in ((up_ref, HALO), (down_ref, HALO + ROWS - 8)):
            rows = slice(base + first, base + first + 8)
            ref[MSG + 8 * i : MSG + 8 * i + 8] = masks_ref[rows]
            ref[MSG + 24 + 8 * i : MSG + 32 + 8 * i] = edge_ref[rows]
    row_even = even("row")
    out_near_ref[...] = jnp.where(row_even, down_ref[...], up_ref[...])
    out_far_ref[...] = jnp.where(row_even, up_ref[...], down_ref[...])


def row_messages(field, masks, near, far, table):
    message = ((MSG + 48, LANES), F32)
    side = ((OWN + 2, HALO, LANES), F32)
    return call(
        rows_kernel, "rows", [message, message, ((256, LANES), F32), side, side], [message, message]
    )(field, masks, near, far, table)


class Stage:
    def __init__(self, first, last, second, load, old, store, rate, weights, S, W, T, group):
        self.first, self.last, self.second = first, last, second
        self.load, self.old, self.store, self.rate = load, old, store, rate
        self.weights, self.S, self.W, self.T, self.group = weights, S, W, T, group

    def mix(self, r, n, keep=None):
        brate, burn, bheat = self.rate
        x = jnp.concatenate([self.load(r + k) for k in range(n)], 0)
        s_all, w_all, tt = mixed(x, self.weights)
        for k in range(n):
            at = slice(k * WIDTH, (k + 1) * WIDTH)
            q = r + k
            rest = None
            self.S[q] = s_all[at]
            self.W[q, 8 : 8 + WIDTH] = w_all[at]
            if self.first <= q < self.last or keep:
                rest = 0.5 * x[at] + (burn(q) * tt[at] + bheat(q))
                self.T[q] = rest
            if q == TILES - 1:
                self.S[q + 1] = pltpu.roll(s_all[at], C, 1)
            if keep:
                keep(q, s_all[at], w_all[at], rest)

    def post(self, q, s_at, w_at, t_at):
        centre = s_at(q) + w_at(q, 8)
        around = (s_at(q - 1) + s_at(q + 1)) + (w_at(q, 7) + w_at(q, 9))
        g = t_at(q) + self.rate[0](q) * (around - centre - centre)
        self.store(q, 0.5 * (self.old(q) + g) if self.second else g)

    def run(self, end, s_at, w_at, t_at, keep=None, before=None):
        r, todo = self.first - 1, self.first
        while r < end:
            n = min(self.group, end - r)
            if 0 < end - r - n < 3:
                n = end - r
            if before:
                before(r + n)
            self.mix(r, n, keep)
            r += n
            limit = self.last if r == end else min(self.last, r - 1)
            for q in range(todo, limit):
                self.post(q, s_at, w_at, t_at)
            todo = max(todo, limit)


def beside(side, own):
    return lambda r: jnp.concatenate([side[r - HALO, 0:8], own[r - HALO], side[r - HALO, 8:16]], 0)


def clear_margins(W):
    W[:, 0:8] = jnp.zeros((W.shape[0], 8, LANES), F32)
    W[:, 8 + WIDTH :] = jnp.zeros((W.shape[0], 8, LANES), F32)


def inner_kernel(
    field_ref, left_ref, right_ref, edge_ref, brate_in, burn_in, bheat_in, table_ref, w1, w2, w3,
    s_in, w_in, t_in, s2_in, w2_in, t2_in, A, B, brate, burn, bheat, kept_s, kept_w, kept_t,
    S, W, T, side_s, side_t, W1, side2_s, side2_t, W2,
):
    clear_margins(W)
    clear_margins(W1)
    clear_margins(W2)
    clear_margins(kept_w)
    for r0 in range(HALO, TILES, 8):
        put_edge_rates(edge_ref, table_ref, r0, HALO, (0, 8), brate, burn, bheat)
    rate = [beside(brate, brate_in), beside(burn, burn_in), beside(bheat, bheat_in)]

    def start(r):
        k = r - HALO
        return jnp.concatenate([left_ref[k], field_ref[k], right_ref[k]], 0)

    x = jnp.concatenate([ref[k] for k in range(OWN) for ref in (left_ref, right_ref)], 0)
    s_all, w_all, tt = mixed(x, (w1, w2, w3))
    for k in range(OWN):
        r, span = HALO + k, slice(16 * k, 16 * k + 16)
        side_s[k] = s_all[span]
        side_t[k] = 0.5 * x[span] + (burn[k] * tt[span] + bheat[k])
        W1[r, 8:16] = w_all[span][0:8]
        W1[r, 16 + COLS : 24 + COLS] = w_all[span][8:16]

        W1[r, 16:32] = w_in[k, 0:16]
        W1[r, COLS : 16 + COLS] = w_in[k, COLS - 16 :]
    W1[HALO, 16 : 16 + COLS] = w_in[0]
    s_of, t_first = beside(side_s, s_in), beside(side_t, t_in)
    parts = (slice(0, 16), slice(COLS, WIDTH))

    def s_first(q):
        return s_of(q) if q < TILES else pltpu.roll(s_of(TILES - 1), C, 1)

    ends = []
    for q in range(HALO + 1, TILES):
        for at in parts:
            a, z = at.start, at.stop
            s_here, t_here, rate_here = s_of(q)[at], t_first(q)[at], rate[0](q)[at]
            centre = s_here + W1[q, a + 8 : z + 8]
            around = (s_first(q - 1)[at] + s_first(q + 1)[at]) + (W1[q, a + 7 : z + 7] + W1[q, a + 9 : z + 9])
            ends.append(t_here + rate_here * (around - centre - centre))
    s_all, w_all, tt = mixed(jnp.concatenate(ends, 0), (w1, w2, w3))
    for q in range(HALO + 1, TILES):
        k, at = q - HALO, slice(32 * (q - HALO - 1), 32 * (q - HALO))
        x = jnp.concatenate(ends[2 * k - 2 : 2 * k], 0)
        burn_here, bheat_here = [jnp.concatenate([rate[i](q)[p] for p in parts], 0) for i in (1, 2)]
        side2_s[k] = s_all[at]
        side2_t[k] = 0.5 * x + (burn_here * tt[at] + bheat_here)
        W2[q, 8:24] = w_all[at][0:16]
        W2[q, 8 + COLS : 24 + COLS] = w_all[at][16:32]

    def second_w(k):
        W2[HALO + k, 24 : 24 + MIDDLE] = w2_in[k]

    def around_middle(side, own):
        return lambda r: jnp.concatenate([side[r - HALO, 0:16], own[r - HALO], side[r - HALO, 16:32]], 0)

    s2_of, t_second = around_middle(side2_s, s2_in), around_middle(side2_t, t2_in)

    def s_second(q):
        return s2_of(q) if q < TILES else pltpu.roll(s2_of(TILES - 1), C, 1)

    def w_second(q, o):
        return W2[q, o : o + WIDTH]

    A[HALO] = start(HALO)
    A[HALO + 1] = start(HALO + 1)
    for s in range(1, STAGES + 1):
        src, dst = (A, B) if s % 2 else (B, A)

        def store(q, value, dst=dst):
            dst[q] = value

        def keep(q, s_value, w_value, t_value, s=s):
            near = q - (HALO + s - 1)
            if near < 2:
                kept_s[s - 1, near] = s_value
            if near == 0:
                kept_w[s - 1, 8 : 8 + WIDTH] = w_value
                kept_t[s - 1] = t_value

        stage = Stage(
            HALO + s, TILES, s % 2 == 0,
            lambda r, src=src: src[r],
            start if s == 2 else (lambda r, dst=dst: dst[r]),
            store, rate, (w1, w2, w3), S, W, T, INNER_GROUP,
        )
        readers = (lambda q: S[q], lambda q, o: W[q, o : o + WIDTH], lambda q: T[q])
        if s == 1:
            for q in (HALO, HALO + 1):
                keep(q, s_first(q), W1[q, 8 : 8 + WIDTH], t_first(q))
            continue
        if s == 2:
            second_w(1)
            second_w(2)
            for q in (HALO + 1, HALO + 2):
                keep(q, s_second(q), W2[q, 8 : 8 + WIDTH], t_second(q))
            opening, finished = stage, [HALO + 2]
            continue

        def before(end):
            for q in range(finished[0], end):
                second_w(q - HALO)
                opening.post(q, s_second, w_second, t_second)
            finished[0] = max(finished[0], end)

        stage.run(TILES, *readers, keep, before if s == 3 else None)


def inner(field, left, right, edge, rate_arrays):
    cells = ((TILES, WIDTH, LANES), F32)
    edges = ((OWN, 2 * HALO, LANES), F32)
    return call(
        inner_kernel, "inner",
        [cells, cells, edges, edges, edges, ((STAGES, 2, WIDTH, LANES), F32),
         ((STAGES, WIDTH + 16, LANES), F32), ((STAGES, WIDTH, LANES), F32)],
        [((TILES + 1, WIDTH, LANES), F32), ((TILES, WIDTH + 16, LANES), F32), cells, edges, edges,
         ((TILES, WIDTH + 16, LANES), F32), ((OWN, 32, LANES), F32), ((OWN, 32, LANES), F32),
         ((TILES, WIDTH + 16, LANES), F32)], limit=24,
    )(field, left, right, edge, *rate_arrays)


def outer_kernel(
    A_in, B_in, brate_side, burn_side, bheat_side, kept_s, kept_w, kept_t, brate_in, burn_in, bheat_in,
    near_ref, far_ref, table_ref, w1, w2, w3,
    out_ref, A, B, brate, burn, bheat, masks, edge, S, W, T,
):
    low = lanes((WIDTH, LANES)) < C
    row_even = even("row")

    def arrived(at):
        near, far = near_ref[at], far_ref[at]
        return jnp.where(row_even, far, near), jnp.where(row_even, near, far)

    for t in range(4):
        top, bottom = arrived(slice(t * WIDTH, (t + 1) * WIDTH))
        A[7 - t] = pltpu.roll(jnp.where(low, bottom, top), C, 1)
        A[3 - t] = jnp.where(low, top, bottom)
    clear_margins(W)
    for i, base in enumerate((FUEL, BURN, LIT)):
        for ref, offset in ((masks, MSG + 8 * i), (edge, MSG + 24 + 8 * i)):
            top, bottom = arrived(slice(offset, offset + 8))
            ref[base : base + 8] = top
            ref[base + HALO + ROWS : base + HEIGHT] = bottom
    for r in range(HALO):
        put_rates(masks, table_ref, r, r, HALO, brate, burn, bheat)
    put_edge_rates(edge, table_ref, 0, 0, (0, HALO + COLS), brate, burn, bheat)

    def reader(near, side, own):
        far = beside(side, own)
        return lambda r: near[r] if r < HALO else far(r)

    rate = [
        reader(brate, brate_side, brate_in), reader(burn, burn_side, burn_in), reader(bheat, bheat_side, bheat_in)
    ]
    for s in range(1, STAGES + 1):
        (src, dst), dst_in = ((A, B), B_in) if s % 2 else ((B, A), A_in)
        edge_tile = HALO + s - 1

        def store(q, value, dst=dst):
            dst[q] = value

        def old(q, dst=dst, dst_in=dst_in, s=s):
            return dst[q] if q < HALO + s - 2 else dst_in[q]

        def load(q, src=src):
            return src[q]

        def s_at(q, e=edge_tile, s=s):
            return S[q] if q < e else kept_s[s - 1, q - e]

        def w_at(q, o, e=edge_tile, s=s):
            return W[q, o : o + WIDTH] if q < e else kept_w[s - 1, o : o + WIDTH]

        def t_at(q, e=edge_tile, s=s):
            return T[q] if q < e else kept_t[s - 1]

        stage = Stage(
            s, HALO + s, s % 2 == 0, load, old, store, rate, (w1, w2, w3), S, W, T, OUTER_GROUP
        )
        stage.run(edge_tile, s_at, w_at, t_at)
    flat = out_ref.reshape(C * ROWS, COLS)
    for k in reversed(range(OWN)):
        r = HALO + k
        turned = (A if r < 2 * HALO else A_in)[r, HALO : HALO + COLS].T
        flat[pl.ds(k, C, stride=ROWS), :] = turned[0:C]
        flat[pl.ds(ROWS - 1 - k, C, stride=ROWS), :] = turned[C:]


def outer(states, rate_arrays, near, far):
    few = 2 * HALO
    cells = ((few, WIDTH, LANES), F32)
    edge_cells = ((HALO, WIDTH, LANES), F32)
    return call(
        outer_kernel, "outer", [((C, ROWS, COLS), F32)],
        [cells, cells, edge_cells, edge_cells, edge_cells, ((192, COLS), F32), ((192, COLS), F32),
         cells, ((few, WIDTH + 16, LANES), F32), cells],
    )(*states, *rate_arrays[:3], near, far, *rate_arrays[3:7])[0]


def exchange(near, far, axis):
    size = lax.axis_size(axis)

    def swap(x, start):
        pairs = [(i, i + 1) for i in range(start, size - 1, 2)]
        return lax.ppermute(x, axis, pairs + [(b, a) for a, b in pairs])

    far = swap(far, 1)
    return swap(near, 0), far


def per_device(
    fire_state, fuel_class, firebreak, ignition,
    spread_rate, spread_rows, spread_cols, reaction, ignition_heat,
):
    field, masks, near, far = pack(fire_state, fuel_class, firebreak, ignition)
    near, far = exchange(near, far, "col")
    rate_arrays = rates(
        masks, spread_rate, ignition_heat[None], spread_rows, spread_cols, reaction, field
    )
    near, far, edge, left, right = row_messages(field, masks, near, far, rate_arrays[3])
    near, far = exchange(near, far, "row")
    states = inner(field, left, right, edge, rate_arrays)
    return outer(states, rate_arrays, near, far)


def solution(mesh):
    whole = P(None, "row", "col")
    cells = P("row", "col")
    return jax.shard_map(
        per_device,
        mesh=mesh,
        in_specs=(whole, cells, cells, cells, P(), P(), P(), P(), P()),
        out_specs=whole,
        check_vma=False,
    )
```

```python
import jax
import jax.numpy as jnp
from jax import lax
from jax.experimental import pallas as pl
from jax.experimental.pallas import tpu as pltpu
from jax.sharding import PartitionSpec as P

ITERS = 4
STAGES = 2 * ITERS
HALO = STAGES
C, ROWS, COLS = 64, 48, 128
HEIGHT = ROWS + 2 * HALO
WIDTH = COLS + 2 * HALO
TILES = HEIGHT // 2
OWN = TILES - HALO
LANES = 2 * C
INNER_GROUP = 8
OUTER_GROUP = 4
MSG = 4 * WIDTH
MIDDLE = COLS - 16
BF = jnp.bfloat16
F32 = jnp.float32


def split(x):
    hi = x.astype(BF)
    return hi, (x - hi.astype(F32)).astype(BF)


def lanes(shape):
    return lax.broadcasted_iota(jnp.int32, shape, len(shape) - 1)


def call(kernel, name, outs, scratch=(), limit=12, from_hbm=0, extra=()):
    specs = {"in_specs": [pl.BlockSpec(memory_space=pltpu.HBM)] * from_hbm} if from_hbm else {}
    return pl.pallas_call(
        kernel,
        name=name,
        out_shape=[jax.ShapeDtypeStruct(s, d) for s, d in outs],
        scratch_shapes=[pltpu.VMEM(s, d) for s, d in scratch] + list(extra),
        **specs,
        compiler_params=pltpu.CompilerParams(vmem_limit_bytes=limit * 2**20),
    )


FUEL, BURN, LIT = 0, HEIGHT, 2 * HEIGHT


def even(axis):
    return lax.rem(lax.axis_index(axis), 2) == 0


def pack_kernel(
    x_hbm, fuel_hbm, break_hbm, lit_hbm, field_ref, masks_ref, near_ref, far_ref, x_ref, ints, sems
):
    copies = [
        pltpu.make_async_copy(x_hbm.at[:, pl.ds(8 * g, 8), :], x_ref.at[:, pl.ds(8 * g, 8), :], sems.at[g])
        for g in range(ROWS // 8)
    ]
    for g in (0, 5, 1, 4, 2, 3):
        copies[g].start()
    small = [
        pltpu.make_async_copy(ref, ints.at[i], sems.at[6 + i])
        for i, ref in enumerate((fuel_hbm, break_hbm, lit_hbm))
    ]
    for copy in small:
        copy.start()
    masks_ref[...] = jnp.zeros_like(masks_ref)
    flat = x_ref.reshape(C * ROWS, COLS)
    is_even = even("col")

    def messages(k, turned):
        first, last = turned[0:HALO], turned[COLS - HALO :]
        near_ref[k] = jnp.where(is_even, last, first)
        far_ref[k] = jnp.where(is_even, first, last)

    for k in range(OWN):
        if k % 8 == 0:
            copies[k // 8].wait()
            copies[5 - k // 8].wait()
        top = flat[pl.ds(k, C, stride=ROWS), :]
        bottom = flat[pl.ds(ROWS - 1 - k, C, stride=ROWS), :]
        turned = jnp.concatenate([top, bottom], 0).T
        field_ref[k] = turned
        messages(k, turned)
    for copy in small:
        copy.wait()
    masks_ref[FUEL + HALO : FUEL + HALO + ROWS] = ints[0].astype(F32)
    masks_ref[BURN + HALO : BURN + HALO + ROWS] = (1 - ints[1]).astype(F32)
    masks_ref[LIT + HALO : LIT + HALO + ROWS] = ints[2].astype(F32)
    messages(OWN, masks_ref[0:128].T)
    messages(OWN + 1, masks_ref[128:256].T)


def pack(x, fuel, firebreak, lit):
    message = ((OWN + 2, HALO, LANES), F32)
    return call(
        pack_kernel, "pack", [((OWN, COLS, LANES), F32), ((256, COLS), F32), message, message],
        [((C, ROWS, COLS), F32)], from_hbm=4,
        extra=[pltpu.VMEM((3, ROWS, COLS), jnp.int32), pltpu.SemaphoreType.DMA((9,))],
    )(*[pltpu.with_memory_space_constraint(a, pltpu.HBM) for a in (x, fuel, firebreak, lit)])


def onehot(fuel, burn, lit):
    slot = lax.broadcasted_iota(jnp.int32, (C, 128), 0)
    cls = (slot & 15).astype(F32)
    halves = []
    for f, b, i in zip(fuel, burn, lit):
        picked = jnp.where((cls == f) | (cls == 13.0), b, jnp.where(cls == 14.0, b * i, 0.0))
        halves.append(jnp.where(slot < 32, picked, 0.0))
    return jnp.concatenate(halves, 0)


def rates_kernel(
    masks_ref, rate_ref, heat_ref, rows_ref, cols_ref, react_ref, field_ref,
    brate_ref, burn_ref, bheat_ref, table_ref, w1_ref, w2_ref, w3_ref, s_ref, w_ref, t_ref,
    s2_ref, w2nd_ref, t2_ref, tab,
):
    tab[...] = jnp.zeros_like(tab)
    tab[0:13, 0:64] = rate_ref[...]
    tab[14:15, 0:64] = heat_ref[...]
    t = tab[...]
    t = t + pltpu.roll(t, 64, 1)
    row = lax.broadcasted_iota(jnp.int32, (16, 128), 0)
    h = jnp.concatenate(
        [jnp.where(row < 13, t, 0.0), jnp.where(row == 13, 1.0, 0.0), jnp.where(row == 14, t, 0.0)], 1
    )
    hi, lo = split(h)
    half = jnp.concatenate([hi.astype(F32), lo.astype(F32), jnp.zeros((32, 384), F32)], 0)
    low = (lanes((64, 384)) & 127) < 64
    table_ref[...] = jnp.concatenate([jnp.where(low, half, 0.0), jnp.where(low, 0.0, half)], 0).astype(BF)

    zero = jnp.zeros((C, C), F32)
    eye = jnp.where(lax.broadcasted_iota(jnp.int32, (C, C), 0) == lanes((C, C)), 1.0, 0.0)

    def both(m):
        return split(jnp.concatenate([jnp.concatenate([m, zero], 1), jnp.concatenate([zero, m], 1)], 0).T)

    r_hi, r_lo = both(rows_ref[...] + eye)
    c_hi, c_lo = both(cols_ref[...] + eye)
    e_hi, e_lo = both(react_ref[...])
    w1_ref[...] = jnp.concatenate([jnp.concatenate([r_hi, c_hi], 1)] * 2, 0)
    w2_ref[...] = jnp.concatenate([r_lo, c_lo], 1)
    w3_ref[...] = jnp.concatenate(
        [jnp.concatenate([e_hi, e_lo], 1), jnp.concatenate([e_hi, jnp.zeros((128, 128), BF)], 1)], 0
    )
    for k in range(OWN):
        put_rates(masks_ref, table_ref, HALO + k, k, 0, brate_ref, burn_ref, bheat_ref)
    for k0 in range(0, OWN, INNER_GROUP):
        x = field_ref[k0 : k0 + INNER_GROUP].reshape(INNER_GROUP * COLS, LANES)
        s_all, w_all, tt = mixed(x, (w1_ref, w2_ref, w3_ref))
        for i in range(INNER_GROUP):
            k, at = k0 + i, slice(i * COLS, (i + 1) * COLS)
            s_ref[k], w_ref[k] = s_all[at], w_all[at]
            t_ref[k] = 0.5 * x[at] + (burn_ref[k] * tt[at] + bheat_ref[k])
    mid = slice(8, 8 + MIDDLE)

    def s_mid(k):
        return s_ref[k, mid] if k < OWN else pltpu.roll(s_ref[OWN - 1, mid], C, 1)

    for k0, n in ((1, 7), (8, 8), (16, 8)):
        xs = []
        for k in range(k0, k0 + n):
            centre = s_mid(k) + w_ref[k, mid]
            around = (s_mid(k - 1) + s_mid(k + 1)) + (w_ref[k, 7 : 7 + MIDDLE] + w_ref[k, 9 : 9 + MIDDLE])
            xs.append(t_ref[k, mid] + brate_ref[k, mid] * (around - centre - centre))
        s_all, w_all, tt = mixed(jnp.concatenate(xs, 0), (w1_ref, w2_ref, w3_ref))
        for i, x in enumerate(xs):
            k, at = k0 + i, slice(i * MIDDLE, (i + 1) * MIDDLE)
            s2_ref[k], w2nd_ref[k] = s_all[at], w_all[at]
            t2_ref[k] = 0.5 * x + (burn_ref[k, mid] * tt[at] + bheat_ref[k, mid])


def mixed(x, weights):
    w1, w2, w3 = weights
    hi, lo = split(x)
    t_hi, t_lo = split(jnp.tanh(x))
    sw = jnp.dot(jnp.concatenate([hi, lo], 1), w1[...], preferred_element_type=F32)
    sw = sw + jnp.dot(hi, w2[...], preferred_element_type=F32)
    tt = jnp.dot(jnp.concatenate([t_hi, t_lo], 1), w3[...], preferred_element_type=F32)
    return sw[:, 0:LANES], sw[:, LANES:], tt[:, 0:LANES] + tt[:, LANES:]


def put_rates(masks_ref, table_ref, r, k, start, brate_ref, burn_ref, bheat_ref):
    pick = lambda base: (masks_ref[base + r : base + r + 1], masks_ref[base + 63 - r : base + 64 - r])
    hot = onehot(pick(FUEL), pick(BURN), pick(LIT)).T.astype(BF)
    got = jnp.dot(hot, table_ref[...], preferred_element_type=F32)
    at = slice(start, start + COLS)
    brate_ref[k, at], burn_ref[k, at], bheat_ref[k, at] = got[:, 0:128], got[:, 128:256], got[:, 256:384]


def put_edge_rates(edge_ref, table_ref, r0, base_r, starts, brate_ref, burn_ref, bheat_ref):
    rows = []
    for base in (FUEL, BURN, LIT):
        halves = []
        for h in range(2):
            total = None
            for k in range(8):
                p = r0 + k if h == 0 else 63 - r0 - k
                part = edge_ref[base + p : base + p + 1]
                part = pltpu.roll(part, 16 * k, 1) if k else part
                total = part if total is None else total + part
            halves.append(total)
        rows.append(halves)
    got = jnp.dot(onehot(*rows).T.astype(BF), table_ref[...], preferred_element_type=F32)
    for k in range(8):
        for side, start in zip((0, 8), starts):
            part = got[16 * k + side : 16 * k + side + 8]
            r, at = r0 + k - base_r, slice(start, start + HALO)
            brate_ref[r, at], burn_ref[r, at], bheat_ref[r, at] = part[:, 0:128], part[:, 128:256], part[:, 256:384]


def rates(masks, rate, heat, rows, cols, react, field):
    cells = ((OWN, COLS, LANES), F32)
    middle = ((OWN, MIDDLE, LANES), F32)
    return call(
        rates_kernel, "rates",
        [cells, cells, cells, ((128, 384), BF), ((256, 256), BF), ((128, 256), BF), ((256, 256), BF),
         cells, cells, cells, middle, middle, middle],
        [((16, 128), F32)],
    )(masks, rate, heat, rows, cols, react, field)


def turned_edges(left_ref, right_ref, k):
    both = jnp.concatenate([left_ref[k], right_ref[k], jnp.zeros((112, 128), F32)], 0)
    return both.T


def rows_kernel(
    field_ref, masks_ref, near_ref, far_ref, table_ref,
    out_near_ref, out_far_ref, edge_ref, left_ref, right_ref, up_ref, down_ref,
):
    is_even = even("col")
    left_ref[...] = jnp.where(is_even, far_ref[...], near_ref[...])
    right_ref[...] = jnp.where(is_even, near_ref[...], far_ref[...])
    low = lanes((WIDTH, LANES)) < C

    def tile(k):
        return jnp.concatenate([left_ref[k], field_ref[k], right_ref[k]], 0)

    for t in range(4):
        near, far = tile(t), pltpu.roll(tile(4 + t), C, 1)
        at = slice(t * WIDTH, (t + 1) * WIDTH)
        up_ref[at] = jnp.where(low, near, far)
        down_ref[at] = jnp.where(low, far, near)
    edge_ref[0:128] = turned_edges(left_ref, right_ref, OWN)
    edge_ref[128:256] = turned_edges(left_ref, right_ref, OWN + 1)
    for i, base in enumerate((FUEL, BURN, LIT)):
        for ref, first in ((up_ref, HALO), (down_ref, HALO + ROWS - 8)):
            rows = slice(base + first, base + first + 8)
            ref[MSG + 8 * i : MSG + 8 * i + 8] = masks_ref[rows]
            ref[MSG + 24 + 8 * i : MSG + 32 + 8 * i] = edge_ref[rows]
    row_even = even("row")
    out_near_ref[...] = jnp.where(row_even, down_ref[...], up_ref[...])
    out_far_ref[...] = jnp.where(row_even, up_ref[...], down_ref[...])


def row_messages(field, masks, near, far, table):
    message = ((MSG + 48, LANES), F32)
    side = ((OWN + 2, HALO, LANES), F32)
    return call(
        rows_kernel, "rows", [message, message, ((256, LANES), F32), side, side], [message, message]
    )(field, masks, near, far, table)


class Stage:
    def __init__(self, first, last, second, load, old, store, rate, weights, S, W, T, group):
        self.first, self.last, self.second = first, last, second
        self.load, self.old, self.store, self.rate = load, old, store, rate
        self.weights, self.S, self.W, self.T, self.group = weights, S, W, T, group

    def mix(self, r, n, keep=None):
        brate, burn, bheat = self.rate
        x = jnp.concatenate([self.load(r + k) for k in range(n)], 0)
        s_all, w_all, tt = mixed(x, self.weights)
        for k in range(n):
            at = slice(k * WIDTH, (k + 1) * WIDTH)
            q = r + k
            rest = None
            self.S[q] = s_all[at]
            self.W[q, 8 : 8 + WIDTH] = w_all[at]
            if self.first <= q < self.last or keep:
                rest = 0.5 * x[at] + (burn(q) * tt[at] + bheat(q))
                self.T[q] = rest
            if q == TILES - 1:
                self.S[q + 1] = pltpu.roll(s_all[at], C, 1)
            if keep:
                keep(q, s_all[at], w_all[at], rest)

    def post(self, q, s_at, w_at, t_at):
        centre = s_at(q) + w_at(q, 8)
        around = (s_at(q - 1) + s_at(q + 1)) + (w_at(q, 7) + w_at(q, 9))
        g = t_at(q) + self.rate[0](q) * (around - centre - centre)
        self.store(q, 0.5 * (self.old(q) + g) if self.second else g)

    def run(self, end, s_at, w_at, t_at, keep=None, before=None):
        r, todo = self.first - 1, self.first
        while r < end:
            n = min(self.group, end - r)
            if 0 < end - r - n < 3:
                n = end - r
            if before:
                before(r + n)
            self.mix(r, n, keep)
            r += n
            limit = self.last if r == end else min(self.last, r - 1)
            for q in range(todo, limit):
                self.post(q, s_at, w_at, t_at)
            todo = max(todo, limit)


def beside(side, own):
    return lambda r: jnp.concatenate([side[r - HALO, 0:8], own[r - HALO], side[r - HALO, 8:16]], 0)


def clear_margins(W):
    W[:, 0:8] = jnp.zeros((W.shape[0], 8, LANES), F32)
    W[:, 8 + WIDTH :] = jnp.zeros((W.shape[0], 8, LANES), F32)


def inner_kernel(
    field_ref, left_ref, right_ref, edge_ref, brate_in, burn_in, bheat_in, table_ref, w1, w2, w3,
    s_in, w_in, t_in, s2_in, w2_in, t2_in, A, B, brate, burn, bheat, kept_s, kept_w, kept_t,
    S, W, T, side_s, side_t, W1, side2_s, side2_t, W2,
):
    clear_margins(W)
    clear_margins(W1)
    clear_margins(W2)
    clear_margins(kept_w)
    for r0 in range(HALO, TILES, 8):
        put_edge_rates(edge_ref, table_ref, r0, HALO, (0, 8), brate, burn, bheat)
    rate = [beside(brate, brate_in), beside(burn, burn_in), beside(bheat, bheat_in)]

    def start(r):
        k = r - HALO
        return jnp.concatenate([left_ref[k], field_ref[k], right_ref[k]], 0)

    x = jnp.concatenate([ref[k] for k in range(OWN) for ref in (left_ref, right_ref)], 0)
    s_all, w_all, tt = mixed(x, (w1, w2, w3))
    for k in range(OWN):
        r, span = HALO + k, slice(16 * k, 16 * k + 16)
        side_s[k] = s_all[span]
        side_t[k] = 0.5 * x[span] + (burn[k] * tt[span] + bheat[k])
        W1[r, 8:16] = w_all[span][0:8]
        W1[r, 16 + COLS : 24 + COLS] = w_all[span][8:16]

        W1[r, 16:32] = w_in[k, 0:16]
        W1[r, COLS : 16 + COLS] = w_in[k, COLS - 16 :]
    W1[HALO, 16 : 16 + COLS] = w_in[0]
    s_of, t_first = beside(side_s, s_in), beside(side_t, t_in)
    parts = (slice(0, 16), slice(COLS, WIDTH))

    def s_first(q):
        return s_of(q) if q < TILES else pltpu.roll(s_of(TILES - 1), C, 1)

    ends = []
    for q in range(HALO + 1, TILES):
        for at in parts:
            a, z = at.start, at.stop
            s_here, t_here, rate_here = s_of(q)[at], t_first(q)[at], rate[0](q)[at]
            centre = s_here + W1[q, a + 8 : z + 8]
            around = (s_first(q - 1)[at] + s_first(q + 1)[at]) + (W1[q, a + 7 : z + 7] + W1[q, a + 9 : z + 9])
            ends.append(t_here + rate_here * (around - centre - centre))
    s_all, w_all, tt = mixed(jnp.concatenate(ends, 0), (w1, w2, w3))
    for q in range(HALO + 1, TILES):
        k, at = q - HALO, slice(32 * (q - HALO - 1), 32 * (q - HALO))
        x = jnp.concatenate(ends[2 * k - 2 : 2 * k], 0)
        burn_here, bheat_here = [jnp.concatenate([rate[i](q)[p] for p in parts], 0) for i in (1, 2)]
        side2_s[k] = s_all[at]
        side2_t[k] = 0.5 * x + (burn_here * tt[at] + bheat_here)
        W2[q, 8:24] = w_all[at][0:16]
        W2[q, 8 + COLS : 24 + COLS] = w_all[at][16:32]

    def second_w(k):
        W2[HALO + k, 24 : 24 + MIDDLE] = w2_in[k]

    def around_middle(side, own):
        return lambda r: jnp.concatenate([side[r - HALO, 0:16], own[r - HALO], side[r - HALO, 16:32]], 0)

    s2_of, t_second = around_middle(side2_s, s2_in), around_middle(side2_t, t2_in)

    def s_second(q):
        return s2_of(q) if q < TILES else pltpu.roll(s2_of(TILES - 1), C, 1)

    def w_second(q, o):
        return W2[q, o : o + WIDTH]

    A[HALO] = start(HALO)
    A[HALO + 1] = start(HALO + 1)
    for s in range(1, STAGES + 1):
        src, dst = (A, B) if s % 2 else (B, A)

        def store(q, value, dst=dst):
            dst[q] = value

        def keep(q, s_value, w_value, t_value, s=s):
            near = q - (HALO + s - 1)
            if near < 2:
                kept_s[s - 1, near] = s_value
            if near == 0:
                kept_w[s - 1, 8 : 8 + WIDTH] = w_value
                kept_t[s - 1] = t_value

        stage = Stage(
            HALO + s, TILES, s % 2 == 0,
            lambda r, src=src: src[r],
            start if s == 2 else (lambda r, dst=dst: dst[r]),
            store, rate, (w1, w2, w3), S, W, T, INNER_GROUP,
        )
        readers = (lambda q: S[q], lambda q, o: W[q, o : o + WIDTH], lambda q: T[q])
        if s == 1:
            for q in (HALO, HALO + 1):
                keep(q, s_first(q), W1[q, 8 : 8 + WIDTH], t_first(q))
            continue
        if s == 2:
            second_w(1)
            second_w(2)
            for q in (HALO + 1, HALO + 2):
                keep(q, s_second(q), W2[q, 8 : 8 + WIDTH], t_second(q))
            opening, finished = stage, [HALO + 2]
            continue

        def before(end):
            for q in range(finished[0], end):
                second_w(q - HALO)
                opening.post(q, s_second, w_second, t_second)
            finished[0] = max(finished[0], end)

        stage.run(TILES, *readers, keep, before if s == 3 else None)


def inner(field, left, right, edge, rate_arrays):
    cells = ((TILES, WIDTH, LANES), F32)
    edges = ((OWN, 2 * HALO, LANES), F32)
    return call(
        inner_kernel, "inner",
        [cells, cells, edges, edges, edges, ((STAGES, 2, WIDTH, LANES), F32),
         ((STAGES, WIDTH + 16, LANES), F32), ((STAGES, WIDTH, LANES), F32)],
        [((TILES + 1, WIDTH, LANES), F32), ((TILES, WIDTH + 16, LANES), F32), cells, edges, edges,
         ((TILES, WIDTH + 16, LANES), F32), ((OWN, 32, LANES), F32), ((OWN, 32, LANES), F32),
         ((TILES, WIDTH + 16, LANES), F32)], limit=24,
    )(field, left, right, edge, *rate_arrays)


def outer_kernel(
    A_in, B_in, brate_side, burn_side, bheat_side, kept_s, kept_w, kept_t, brate_in, burn_in, bheat_in,
    near_ref, far_ref, table_ref, w1, w2, w3,
    out_ref, A, B, brate, burn, bheat, masks, edge, S, W, T,
):
    low = lanes((WIDTH, LANES)) < C
    row_even = even("row")

    def arrived(at):
        near, far = near_ref[at], far_ref[at]
        return jnp.where(row_even, far, near), jnp.where(row_even, near, far)

    for t in range(4):
        top, bottom = arrived(slice(t * WIDTH, (t + 1) * WIDTH))
        A[7 - t] = pltpu.roll(jnp.where(low, bottom, top), C, 1)
        A[3 - t] = jnp.where(low, top, bottom)
    clear_margins(W)
    for i, base in enumerate((FUEL, BURN, LIT)):
        for ref, offset in ((masks, MSG + 8 * i), (edge, MSG + 24 + 8 * i)):
            top, bottom = arrived(slice(offset, offset + 8))
            ref[base : base + 8] = top
            ref[base + HALO + ROWS : base + HEIGHT] = bottom
    for r in range(HALO):
        put_rates(masks, table_ref, r, r, HALO, brate, burn, bheat)
    put_edge_rates(edge, table_ref, 0, 0, (0, HALO + COLS), brate, burn, bheat)

    flat = out_ref.reshape(C * ROWS, COLS)

    def put_out(k, state):
        turned = state[HALO + k, HALO : HALO + COLS].T
        flat[pl.ds(k, C, stride=ROWS), :] = turned[0:C]
        flat[pl.ds(ROWS - 1 - k, C, stride=ROWS), :] = turned[C:]

    def reader(near, side, own):
        far = beside(side, own)
        return lambda r: near[r] if r < HALO else far(r)

    rate = [
        reader(brate, brate_side, brate_in), reader(burn, burn_side, burn_in), reader(bheat, bheat_side, bheat_in)
    ]
    for s in range(1, STAGES + 1):
        (src, dst), dst_in = ((A, B), B_in) if s % 2 else ((B, A), A_in)
        edge_tile = HALO + s - 1

        def store(q, value, dst=dst):
            dst[q] = value

        def old(q, dst=dst, dst_in=dst_in, s=s):
            return dst[q] if q < HALO + s - 2 else dst_in[q]

        def load(q, src=src):
            return src[q]

        def s_at(q, e=edge_tile, s=s):
            return S[q] if q < e else kept_s[s - 1, q - e]

        def w_at(q, o, e=edge_tile, s=s):
            return W[q, o : o + WIDTH] if q < e else kept_w[s - 1, o : o + WIDTH]

        def t_at(q, e=edge_tile, s=s):
            return T[q] if q < e else kept_t[s - 1]

        stage = Stage(
            s, HALO + s, s % 2 == 0, load, old, store, rate, (w1, w2, w3), S, W, T, OUTER_GROUP
        )
        stage.run(edge_tile, s_at, w_at, t_at)
        put_out(HALO + 2 * s - 2, A_in)
        put_out(HALO + 2 * s - 1, A_in)
    for k in range(HALO):
        put_out(k, A)


def outer(states, rate_arrays, near, far):
    few = 2 * HALO
    cells = ((few, WIDTH, LANES), F32)
    edge_cells = ((HALO, WIDTH, LANES), F32)
    return call(
        outer_kernel, "outer", [((C, ROWS, COLS), F32)],
        [cells, cells, edge_cells, edge_cells, edge_cells, ((192, COLS), F32), ((192, COLS), F32),
         cells, ((few, WIDTH + 16, LANES), F32), cells],
    )(*states, *rate_arrays[:3], near, far, *rate_arrays[3:7])[0]


def exchange(near, far, axis):
    size = lax.axis_size(axis)

    def swap(x, start):
        pairs = [(i, i + 1) for i in range(start, size - 1, 2)]
        return lax.ppermute(x, axis, pairs + [(b, a) for a, b in pairs])

    far = swap(far, 1)
    return swap(near, 0), far


def per_device(
    fire_state, fuel_class, firebreak, ignition,
    spread_rate, spread_rows, spread_cols, reaction, ignition_heat,
):
    field, masks, near, far = pack(fire_state, fuel_class, firebreak, ignition)
    near, far = exchange(near, far, "col")
    rate_arrays = rates(
        masks, spread_rate, ignition_heat[None], spread_rows, spread_cols, reaction, field
    )
    near, far, edge, left, right = row_messages(field, masks, near, far, rate_arrays[3])
    near, far = exchange(near, far, "row")
    states = inner(field, left, right, edge, rate_arrays)
    return outer(states, rate_arrays, near, far)


def solution(mesh):
    whole = P(None, "row", "col")
    cells = P("row", "col")
    return jax.shard_map(
        per_device,
        mesh=mesh,
        in_specs=(whole, cells, cells, cells, P(), P(), P(), P(), P()),
        out_specs=whole,
        check_vma=False,
    )
```
